256 devices in a mesh: mem: 16 (over x, y), reach: 16 (over z, core).
Axes of the slice: x: 4, y: 4, z: 8, core: 2. Of those that a mesh axis runs over, the one named last changes fastest.
Arguments:
- ensemble: float32 [256, 48, 32768], P('mem', None, 'reach'), may hold values from -6 to 6
- outgoing_fraction: float32 [48, 32768], P(None, 'reach'), may hold values from 0.1 to 0.5
- mixing: float32 [48, 48], replicated, may hold values from -0.875 to 0.875
- downstream_position: int32 [32768], P('reach'), may hold values from 0 to 256, as said below
- obs_index: int32 [256, 256], P('reach'), may hold values from 0 to 6143
- obs_value: float32 [256, 256], P('reach'), may hold values from -6 to 6
- obs_error: float32 [256, 256], P('reach'), may hold values from 0.5 to 2
- obs_count: int32 [256], P('reach'), may hold values from 1 to 256, 39321 in all
Outputs:
- analysis: float32 [256, 48, 32768], P('mem', None, 'reach')
The draws below stay inside these ranges and needn't reach their ends.
Inputs may be any that keep to these rules, and one draw needn't show every extreme that they name: `downstream_position`: A value v below 128 points into the reach's own block, v from 128 to 255 to reach v - 128 of the next block, 256 means the reach drains out; a reach never drains into itself, and reaches of the last block never drain into a next block.
All inputs are finite; a program needn't handle non-finite values. No bound on the sum of `obs_count` on one device may be relied on, other than what follows from the above.
Results may differ from the reference program's by a relative error of at most 0.0003.
Values sent between devices are 32-bit elements; how exact they have to be, the bound alone decides.
No kernel may reach another device: no remote copies, remote signals or barrier semaphores. Data moves between devices by JAX's collectives and lax.ppermute only.
A program may use at most 192 MiB of HBM per device.

```python
import math
import jax
import jax.numpy as jnp
import numpy as np
from jax import lax

K = 256
S = 48
BL = 128
OCAP = 256
SUBSTEPS = 2
NBLK = 256
R = 32768


def draw_downstream_position(key, part):
    key = jax.random.fold_in(key, 11)
    positions = jnp.arange(R, dtype=jnp.int32)
    within = positions % BL
    block_of = positions // BL
    drawn = jax.random.randint(key, (R,), 0, 2 * BL + 1, dtype=jnp.int32)
    drawn = jnp.where(drawn == within, 2 * BL, drawn)
    last_block = block_of == R // BL - 1
    drawn = jnp.where(last_block & (drawn >= BL), 2 * BL, drawn)
    drawn = jnp.where(within == 1, 0, drawn)
    drawn = jnp.where(last_block & (within == 0), 2 * BL, drawn)
    return drawn.astype(jnp.int32)


def with_ends(result, stream_key, least, top_value):
    longest = result.shape.index(max(result.shape))
    spots = []
    for shift in (0, 1):
        where = [jax.random.randint(jax.random.fold_in(stream_key, axis), (), 0, length) for axis, length in enumerate(result.shape)]
        where[longest] = (where[longest] + shift) % result.shape[longest]
        spots.append(tuple(where))
    return result.at[spots[0]].set(least).at[spots[1]].set(top_value)


def block_scale(key, shape, split, smallest, top_value):
    level = 1.0
    for position, shards_of in split:
        steps = jax.random.uniform(jax.random.fold_in(jax.random.fold_in(key, 6), position), (shards_of,), jnp.float32, smallest / len(split), top_value / len(split))
        level = level * jnp.repeat(jnp.exp(steps), shape[position] // shards_of).reshape((-1,) + (1,) * (len(shape) - 1 - position))
    return level


def length_profile(count, total, bound, lean):
    portions = [(1 << 20) // math.isqrt(grade ** lean) + 1 for grade in range(2, count + 1)]
    rest, given = total - bound - (count - 1), [1] * (count - 1)
    while rest > 0:
        movable = [i for i in range(count - 1) if given[i] < bound]
        pool, budget = sum([portions[i] for i in movable]), rest
        for i in movable:
            addition = min(bound - given[i], max(1, budget * portions[i] // pool), rest)
            given[i] = given[i] + addition
            rest = rest - addition
    return np.array([bound] + given)


def ragged(stream_key, amount, total, most, lean):
    if amount == 2:
        one = jax.random.randint(stream_key, (), max(1, total - most), min(most, total - 1) + 1)
        return jnp.stack([one, total - one])
    lengths = jnp.asarray(length_profile(amount, total, most, lean), jnp.int32)
    twos = (amount - 1) // 2
    giver, receiver = lengths[1:1 + 2 * twos:2], lengths[2:2 + 2 * twos:2]
    room = jnp.minimum(giver - 1, most - receiver)
    passed = jax.random.randint(jax.random.fold_in(stream_key, 1), (twos,), 0, 1 << 20) % (room + 1)
    lengths = lengths.at[1:1 + 2 * twos:2].set(giver - passed).at[2:2 + 2 * twos:2].set(receiver + passed)
    return lengths[jax.random.permutation(jax.random.fold_in(stream_key, 2), amount)]


def normal_values(own_key, shape, scale, reach, shards=(), held_as=jnp.bfloat16):
    values = jax.random.normal(own_key, shape, jnp.float32) * scale
    if len(shards) > 0:
        values = block_scale(own_key, shape, shards, -0.22, 0.18) * values
    return jnp.clip(values, min=-reach, max=reach).astype(held_as)


def setup_inputs(seed: int = 0) -> dict:
    splits = jax.random.split(jax.random.key(seed), 9)
    ensemble = normal_values(splits[0], (K, S, R), 1.0, 6.0, ((0, 16), (2, 16)), jnp.float32)
    outgoing_fraction = jnp.clip(jnp.exp(math.log(0.5) - 1.609438 * jax.random.uniform(splits[1], (S, R), jnp.float32) ** block_scale(splits[1], (S, R), ((1, 16),), -0.2, 0.2)), 0.1, 0.5)
    mixing = normal_values(splits[2], (S, S), S ** -0.5, 0.875, (), jnp.float32)
    downstream_position = draw_downstream_position(jax.random.fold_in(splits[8], 71), 0)
    obs_index = with_ends(jax.random.randint(splits[4], (NBLK, OCAP), 0, S * BL), jax.random.fold_in(splits[4], 1), 0, (S * BL) - 1).astype(jnp.int32)
    obs_value = normal_values(splits[5], (NBLK, OCAP), 1.0, 6.0, ((0, 16),), jnp.float32)
    obs_error = jnp.clip(jnp.exp(math.log(2.0) - 1.3862944 * jax.random.uniform(splits[6], (NBLK, OCAP), jnp.float32) ** block_scale(splits[6], (NBLK, OCAP), ((0, 16),), -0.2, 0.2)), 0.5, 2.0)
    obs_count = ragged(splits[7], NBLK, NBLK * OCAP * 3 // 5, OCAP, 2).astype(jnp.int32)
    return dict(ensemble=ensemble, outgoing_fraction=outgoing_fraction, mixing=mixing, downstream_position=downstream_position, obs_index=obs_index, obs_value=obs_value, obs_error=obs_error, obs_count=obs_count)


def route_substep(present_state, outgoing_fraction, mixing, targets):
    outflow = outgoing_fraction[None] * present_state
    spill = jnp.zeros((K, S, R + 1), jnp.float32).at[:, :, targets].add(outflow)
    inflow = spill[:, :, :R]
    blending_term = jnp.einsum('ts,ktr->ksr', mixing, present_state, precision=lax.Precision.HIGHEST)
    return present_state - outflow + inflow + 0.5 * jnp.tanh(blending_term)

def innovation_terms(observed, values, errors, count):
    slots = observed.shape[1]
    live_mask = (jnp.arange(slots, dtype=jnp.int32) < count).astype(jnp.float32)
    obs_mean = lax.optimization_barrier(jnp.mean(observed, axis=0))
    obs_pert = observed - obs_mean[None]
    spread = lax.optimization_barrier(jnp.sum(obs_pert * obs_pert, axis=0)) / (K - 1)
    departure = values - obs_mean
    statistic = jnp.sum(live_mask * departure * departure / (errors * errors + spread))
    return (obs_pert, departure, live_mask, statistic)

def transform_matrix(obs_pert, departure, live_mask, errors, inflation):
    ensemble_runs = obs_pert.shape[0]
    weight_row = live_mask / (errors * errors)
    weighted = obs_pert * weight_row[None]
    identity = jnp.eye(ensemble_runs, dtype=jnp.float32)
    system = jnp.dot(weighted, obs_pert.T, precision=lax.Precision.HIGHEST) + (K - 1) / inflation * identity
    lower_factor = jnp.linalg.cholesky(system)
    inverse_lower = jax.scipy.linalg.solve_triangular(lower_factor, identity, lower=True)
    right_side = jnp.dot(weighted, departure, precision=lax.Precision.HIGHEST)
    half_way = jnp.dot(inverse_lower, right_side, precision=lax.Precision.HIGHEST)
    mean_weight = jnp.dot(inverse_lower.T, half_way, precision=lax.Precision.HIGHEST)
    return mean_weight[:, None] + jnp.sqrt(jnp.float32(K - 1)) * inverse_lower.T

def apply_transform(block_state, mixer):
    ens_mean = lax.optimization_barrier(jnp.mean(block_state, axis=0))
    ens_pert = block_state - ens_mean[None]
    moved = jnp.einsum('jk,jsr->ksr', mixer, ens_pert, precision=lax.Precision.HIGHEST)
    return ens_mean[None] + moved

def reference(ensemble, outgoing_fraction, mixing, downstream_position, obs_index, obs_value, obs_error, obs_count):
    positions = jnp.arange(R, dtype=jnp.int32)
    block_of = positions // BL
    targets = jnp.where(downstream_position < 2 * BL, block_of * BL + downstream_position, R).astype(jnp.int32)
    present_state = ensemble
    for substep in range(SUBSTEPS):
        present_state = route_substep(present_state, outgoing_fraction, mixing, targets)
    blocks_view = jnp.moveaxis(present_state.reshape(K, S, NBLK, BL), 2, 0)

    def first_pass(packed):
        block_state, slots, values, errors, count = packed
        observed = block_state.reshape(K, S * BL)[:, slots]
        return innovation_terms(observed, values, errors, count)[3]
    stats = lax.map(first_pass, (blocks_view, obs_index, obs_value, obs_error, obs_count))
    inflation = 0.5 + jnp.sum(stats) / jnp.sum(obs_count.astype(jnp.float32))

    def second_pass(packed):
        block_state, slots, values, errors, count = packed
        observed = block_state.reshape(K, S * BL)[:, slots]
        obs_pert, departure, live_mask, statistic = innovation_terms(observed, values, errors, count)
        mixer = transform_matrix(obs_pert, departure, live_mask, errors, inflation)
        return apply_transform(block_state, mixer)
    updated = lax.map(second_pass, (blocks_view, obs_index, obs_value, obs_error, obs_count))
    return jnp.moveaxis(updated, 0, 2).reshape(K, S, R)
```

```python
import jax
import jax.numpy as jnp
from jax import lax
from jax.experimental import pallas as pl
from jax.experimental.pallas import tpu as pltpu
from jax.sharding import PartitionSpec as P

BL = 128
HIGHEST = lax.Precision.HIGHEST
NT = (((1,), (1,)), ((), ()))
NN = (((1,), (0,)), ((), ()))
TN = (((0,), (0,)), ((), ()))
VMEM_LIMIT = 48 * 1024 * 1024


def dot(a, b, dims=NN):
    return lax.dot_general(a, b, dims, precision=HIGHEST, preferred_element_type=jnp.float32)


def fast_dot(a, b, dims=NN):
    return lax.dot_general(a, b, dims, preferred_element_type=jnp.float32)


def halves(x):
    high = x.astype(jnp.bfloat16)
    low = (x - high.astype(jnp.float32)).astype(jnp.bfloat16)
    return high, low


def selector(index_row, size):
    rows = lax.broadcasted_iota(jnp.int32, (size, index_row.shape[1]), 0)
    hot = (rows == index_row).astype(jnp.float32).astype(jnp.bfloat16)
    return jnp.concatenate([hot, hot], axis=1)


def select(x, table):
    m, s, r = x.shape
    high, low = halves(x.reshape(m * s, r))
    out = fast_dot(jnp.concatenate([high, low], axis=1), table, NT)
    return out.reshape(m, s, table.shape[0])


def blend(x, mix3):
    parts = []
    for k in range(0, x.shape[0], 2):
        pair = jnp.concatenate([x[k], x[k + 1]], axis=1)
        high, low = halves(pair)
        out = fast_dot(mix3, jnp.concatenate([high, low, high], axis=0))
        parts += [out[:, :BL], out[:, BL:]]
    return 0.5 * jnp.tanh(jnp.stack(parts))


def prepare_mixing(mixing_ref, mix3_ref):
    s = mixing_ref.shape[0]
    rows = lax.broadcasted_iota(jnp.int32, (s, s), 0)
    cols = lax.broadcasted_iota(jnp.int32, (s, s), 1)
    flipped = dot(mixing_ref[...], (rows == cols).astype(jnp.float32), TN)
    high, low = halves(flipped)
    mix3_ref[...] = jnp.concatenate([high, high, low], axis=1)


def edge_kernel(x_ref, f_ref, v_ref, mixing_ref, c1_ref, c2_ref, mix3_ref):
    prepare_mixing(mixing_ref, mix3_ref)
    outflow = f_ref[:, :BL][None] * x_ref[:, :, :BL]
    c1_before = select(outflow, selector(v_ref[:, :BL], 2 * BL))[:, :, BL:]
    table = selector(v_ref[:, BL:], 2 * BL)
    x = x_ref[:, :, BL:]
    f = f_ref[:, BL:][None]
    outflow = f * x
    routed = select(outflow, table)
    c1_ref[...] = routed[:, :, BL:]
    x = x - outflow + (routed[:, :, :BL] + c1_before) + blend(x, mix3_ref[...])
    c2_ref[...] = select(f * x, table)[:, :, BL:]


def edge_carries(ensemble, fraction, positions, mixing, pair):
    m, s, _ = ensemble.shape
    carry = jax.ShapeDtypeStruct((m, s, BL), jnp.float32)
    return pl.pallas_call(
        edge_kernel,
        grid=(1,),
        in_specs=[
            pl.BlockSpec((m, s, 2 * BL), lambda g: (0, 0, pair)),
            pl.BlockSpec((s, 2 * BL), lambda g: (0, pair)),
            pl.BlockSpec((1, 2 * BL), lambda g: (0, pair)),
            pl.BlockSpec((s, s), lambda g: (0, 0)),
        ],
        out_specs=[pl.BlockSpec((m, s, BL), lambda g: (0, 0, 0))] * 2,
        out_shape=[carry, carry],
        scratch_shapes=[pltpu.VMEM((s, 3 * s), jnp.bfloat16)],
        compiler_params=pltpu.CompilerParams(vmem_limit_bytes=VMEM_LIMIT),
        name="edge",
    )(ensemble, fraction, positions, mixing)


def forecast_kernel(
    x_ref, f_ref, v_ref, mixing_ref, slot_ref, c1_in, c2_in, *rest
):
    out_ref, seen_ref, mix3_ref, c1_ref, c2_ref = rest[-5:]

    @pl.when(pl.program_id(0) == 0)
    def _():
        prepare_mixing(mixing_ref, mix3_ref)
        c1_ref[...] = c1_in[...]
        c2_ref[...] = c2_in[...]

    table = selector(v_ref[...], 2 * BL)
    f = f_ref[...][None]
    x = x_ref[...]
    for carry in (c1_ref, c2_ref):
        outflow = f * x
        routed = select(outflow, table)
        x = x - outflow + (routed[:, :, :BL] + carry[...]) + blend(x, mix3_ref[...])
        carry[...] = routed[:, :, BL:]
    out_ref[...] = x[None]
    slots = slot_ref[0]
    m, s, _ = x.shape
    state_of = slots // BL
    reach_of = slots - state_of * BL
    hot_reach = selector_columns(reach_of)
    looked = select(x, hot_reach)
    rows = lax.broadcasted_iota(jnp.int32, (s, slots.shape[1]), 0)
    hot_state = (rows == state_of).astype(jnp.float32)
    seen_ref[...] = jnp.sum(looked * hot_state[None], axis=1)[None]


def selector_columns(reach_row):
    slots = reach_row.shape[1]
    rows = lax.broadcasted_iota(jnp.int32, (BL, slots), 0)
    hot = (rows == reach_row).astype(jnp.float32)
    hot = hot.T.astype(jnp.bfloat16)
    return jnp.concatenate([hot, hot], axis=1)


def forecast_blocks(ensemble, fraction, positions, mixing, slots, c1, c2, first, number, held=None):
    m, s, r = ensemble.shape
    blocks = r // BL
    cap = slots.shape[-1]
    whole = lambda *shape: pl.BlockSpec(shape, lambda g: (0,) * len(shape))
    in_specs = [
        pl.BlockSpec((m, s, BL), lambda g: (0, 0, g + first)),
        pl.BlockSpec((s, BL), lambda g: (0, g + first)),
        pl.BlockSpec((1, BL), lambda g: (0, g + first)),
        whole(s, s),
        pl.BlockSpec((1, 1, cap), lambda g: (g + first, 0, 0)),
        whole(m, s, BL),
        whole(m, s, BL),
    ]
    operands = [ensemble, fraction, positions, mixing, slots, c1, c2]
    aliases = {}
    if held is not None:
        in_specs += [pl.BlockSpec(memory_space=pl.ANY)] * 2
        operands += list(held)
        aliases = {7: 0, 8: 1}
    return pl.pallas_call(
        forecast_kernel,
        grid=(number,),
        in_specs=in_specs,
        out_specs=[
            pl.BlockSpec((1, m, s, BL), lambda g: (g + first, 0, 0, 0)),
            pl.BlockSpec((1, m, cap), lambda g: (g + first, 0, 0)),
        ],
        out_shape=[
            jax.ShapeDtypeStruct((blocks, m, s, BL), jnp.float32),
            jax.ShapeDtypeStruct((blocks, m, cap), jnp.float32),
        ],
        scratch_shapes=[
            pltpu.VMEM((s, 3 * s), jnp.bfloat16),
            pltpu.VMEM((m, s, BL), jnp.float32),
            pltpu.VMEM((m, s, BL), jnp.float32),
        ],
        input_output_aliases=aliases,
        compiler_params=pltpu.CompilerParams(vmem_limit_bytes=VMEM_LIMIT),
        name="forecast",
    )(*operands)


def innovation_kernel(seen_ref, values_ref, errors_ref, count_ref, gram_ref, right_ref, sums_ref):
    seen = seen_ref[...]
    runs, cap = seen.shape
    count = count_ref[0, 0]
    live = (lax.broadcasted_iota(jnp.int32, (1, cap), 1) < count).astype(jnp.float32)
    mean = jnp.sum(seen, axis=0, keepdims=True) * (1.0 / runs)
    pert = seen - mean
    spread = jnp.sum(pert * pert, axis=0, keepdims=True) / (runs - 1)
    errors = errors_ref[...]
    departure = values_ref[...] - mean
    squared = errors * errors
    statistic = jnp.sum(live * departure * departure / (squared + spread), axis=1, keepdims=True)
    weight = live / squared
    weighted = pert * weight
    gram_ref[...] = dot(weighted, pert, NT)
    right_ref[...] = dot(jnp.broadcast_to(departure, (8, cap)), weighted, NT)
    lanes = lax.broadcasted_iota(jnp.int32, sums_ref.shape, 1)
    sums_ref[...] = jnp.where(lanes < 64, statistic, count.astype(jnp.float32))


def innovations(seen, values, errors, count):
    runs, cap = seen.shape
    vmem = pl.BlockSpec(memory_space=pltpu.VMEM)
    return pl.pallas_call(
        innovation_kernel,
        in_specs=[vmem, vmem, vmem, pl.BlockSpec(memory_space=pltpu.SMEM)],
        out_specs=[vmem] * 3,
        out_shape=[
            jax.ShapeDtypeStruct((runs, runs), jnp.float32),
            jax.ShapeDtypeStruct((8, runs), jnp.float32),
            jax.ShapeDtypeStruct((8, 128), jnp.float32),
        ],
        name="innovation",
    )(seen, values, errors, count)


def small_inverse_factor(a):
    n = a.shape[0]
    rows = lax.broadcasted_iota(jnp.int32, (n, n), 0)
    cols = lax.broadcasted_iota(jnp.int32, (n, n), 1)
    eye = (rows == cols).astype(jnp.float32)
    both = jnp.concatenate([a, eye], axis=1)
    below = lax.broadcasted_iota(jnp.int32, (n, 1), 0)
    scales = jnp.zeros((n, 1), jnp.float32)
    for j in range(n):
        pivot = both[j : j + 1, j : j + 1]
        row = both[j : j + 1, :] * (1.0 / pivot)
        factor = jnp.where(below > j, both[:, j : j + 1], 0.0)
        scales = jnp.where(below == j, pivot, scales)
        both = both - factor * row
    return both[:, n:] * (1.0 / jnp.sqrt(scales))


def inverse_factor(a):
    n = a.shape[0]
    if n <= 32:
        return small_inverse_factor(a)
    h = n // 2
    first = inverse_factor(a[:h, :h])
    cross = dot(a[h:, :h], first, NT)
    second = inverse_factor(a[h:, h:] - dot(cross, cross, NT))
    lower = -dot(second, dot(cross, first))
    zero = jnp.zeros((h, h), jnp.float32)
    return jnp.concatenate(
        [jnp.concatenate([first, zero], axis=1), jnp.concatenate([lower, second], axis=1)], axis=0
    )


def mixer_kernel(gram_ref, right_ref, sums_ref, mixer_ref):
    runs = gram_ref.shape[0]
    inflation = 0.5 + sums_ref[0:1, 0:1] / sums_ref[0:1, 64:65]
    rows = lax.broadcasted_iota(jnp.int32, (runs, runs), 0)
    cols = lax.broadcasted_iota(jnp.int32, (runs, runs), 1)
    system = gram_ref[...] + jnp.where(rows == cols, (runs - 1) / inflation, 0.0)
    inverse = inverse_factor(system)
    half_way = dot(right_ref[...], inverse, NT)
    mean_weight = dot(half_way, inverse)
    mixer_ref[...] = mean_weight[0:1] + jnp.sqrt(jnp.float32(runs - 1)) * inverse


def mixer_of(gram, right, sums):
    vmem = pl.BlockSpec(memory_space=pltpu.VMEM)
    return pl.pallas_call(
        mixer_kernel,
        in_specs=[vmem] * 3,
        out_specs=vmem,
        out_shape=jax.ShapeDtypeStruct(gram.shape, jnp.float32),
        compiler_params=pltpu.CompilerParams(vmem_limit_bytes=VMEM_LIMIT),
        name="mixer",
    )(gram, right, sums)


def apply_kernel(mixer_ref, x_ref, out_ref):
    runs, states, lanes = x_ref.shape
    high, low = halves(mixer_ref[...])
    wide = jnp.concatenate([high, low, high], axis=1)
    x_rows = x_ref.reshape(runs * states, lanes)
    out_rows = out_ref.reshape(runs * states, lanes)
    for s in range(0, states, 2):
        x = jnp.concatenate(
            [x_rows[pl.ds(s + i, runs, stride=states), :] for i in range(2)], axis=1
        )
        mean = jnp.sum(x, axis=0, keepdims=True) * (1.0 / runs)
        x_high, x_low = halves(x - mean)
        out = mean + fast_dot(wide, jnp.concatenate([x_high, x_high, x_low], axis=0))
        for i in range(2):
            out_rows[pl.ds(s + i, runs, stride=states), :] = out[:, i * lanes : (i + 1) * lanes]


def apply_mixer(mixer, x):
    runs, states, lanes = x.shape
    chunk = 8
    block = pl.BlockSpec((runs, chunk, lanes), lambda g: (0, g, 0))
    return pl.pallas_call(
        apply_kernel,
        grid=(states // chunk,),
        in_specs=[pl.BlockSpec((runs, runs), lambda g: (0, 0)), block],
        out_specs=block,
        out_shape=jax.ShapeDtypeStruct(x.shape, jnp.float32),
        compiler_params=pltpu.CompilerParams(vmem_limit_bytes=VMEM_LIMIT),
        name="apply",
    )(mixer, x)


def unpack_kernel(x_ref, out_ref):
    for b in range(x_ref.shape[0]):
        out_ref[:, :, b * BL : (b + 1) * BL] = x_ref[b]


def unpack(x):
    blocks, m, s, lanes = x.shape
    return pl.pallas_call(
        unpack_kernel,
        grid=(m // 2,),
        in_specs=[pl.BlockSpec((blocks, 2, s, lanes), lambda g: (0, g, 0, 0))],
        out_specs=pl.BlockSpec((2, s, blocks * lanes), lambda g: (g, 0, 0)),
        out_shape=jax.ShapeDtypeStruct((m, s, blocks * lanes), jnp.float32),
        compiler_params=pltpu.CompilerParams(vmem_limit_bytes=VMEM_LIMIT),
        name="unpack",
    )(x)


def butterfly_sum(x, axes):
    for axis in axes:
        size = lax.axis_size(axis)
        step = 1
        while step < size:
            x = x + lax.ppermute(x, axis, [(i, i ^ step) for i in range(size)])
            step *= 2
    return x


def on_device(
    ensemble,
    outgoing_fraction,
    mixing,
    downstream_position,
    obs_index,
    obs_value,
    obs_error,
    obs_count,
):
    m, s, r = ensemble.shape
    blocks = r // BL
    cap = obs_index.shape[1]
    mem_index = lax.axis_index("mem")
    reaches = lax.axis_size("reach")
    positions = downstream_position.reshape(1, r)
    slots = obs_index.reshape(blocks, 1, cap)
    values = lax.dynamic_slice_in_dim(obs_value, mem_index, 1, 0)
    errors = lax.dynamic_slice_in_dim(obs_error, mem_index, 1, 0)
    count = lax.dynamic_slice_in_dim(obs_count, mem_index, 1, 0).reshape(1, 1)

    routing = (ensemble, outgoing_fraction, positions, mixing)
    route = [(i, i + 1) for i in range(reaches - 1)]
    halo = [lax.ppermute(c, "reach", route) for c in edge_carries(*routing, blocks // 2 - 1)]
    inner = edge_carries(*routing, 0)
    held = forecast_blocks(*routing, slots, *inner, 2, blocks - 2)
    forecast, seen = forecast_blocks(*routing, slots, *halo, 0, 2, held)

    seen = lax.all_to_all(seen, "mem", split_axis=0, concat_axis=0, tiled=True)
    gathered = lax.all_to_all(forecast, "mem", split_axis=0, concat_axis=0, tiled=True)
    runs = blocks * m
    gram, right, sums = innovations(seen.reshape(runs, cap), values, errors, count)
    sums = butterfly_sum(sums, ("reach", "mem"))
    mixer = mixer_of(gram, right, sums)
    updated = apply_mixer(mixer, gathered.reshape(runs, s, BL))
    returned = lax.all_to_all(
        updated.reshape(blocks, m, s, BL), "mem", split_axis=0, concat_axis=0, tiled=True
    )
    return unpack(returned)


def solution(mesh):
    placed = (
        P("mem", None, "reach"),
        P(None, "reach"),
        P(),
        P("reach"),
        P("reach", None),
        P("reach", None),
        P("reach", None),
        P("reach"),
    )
    return jax.shard_map(
        on_device, mesh=mesh, in_specs=placed, out_specs=P("mem", None, "reach"), check_vma=False
    )
```

```python
import jax
import jax.numpy as jnp
from jax import lax
from jax.experimental import pallas as pl
from jax.experimental.pallas import tpu as pltpu
from jax.sharding import PartitionSpec as P

BL = 128
HIGHEST = lax.Precision.HIGHEST
NT = (((1,), (1,)), ((), ()))
NN = (((1,), (0,)), ((), ()))
TN = (((0,), (0,)), ((), ()))
VMEM_LIMIT = 48 * 1024 * 1024


def dot(a, b, dims=NN):
    return lax.dot_general(a, b, dims, precision=HIGHEST, preferred_element_type=jnp.float32)


def fast_dot(a, b, dims=NN):
    return lax.dot_general(a, b, dims, preferred_element_type=jnp.float32)


def halves(x):
    high = x.astype(jnp.bfloat16)
    low = (x - high.astype(jnp.float32)).astype(jnp.bfloat16)
    return high, low


def selector(index_row, size):
    rows = lax.broadcasted_iota(jnp.int32, (size, index_row.shape[1]), 0)
    hot = (rows == index_row).astype(jnp.float32).astype(jnp.bfloat16)
    return jnp.concatenate([hot, hot], axis=1)


def select(x, table):
    m, s, r = x.shape
    high, low = halves(x.reshape(m * s, r))
    out = fast_dot(jnp.concatenate([high, low], axis=1), table, NT)
    return out.reshape(m, s, table.shape[0])


def blend(x, mix3):
    parts = []
    for k in range(0, x.shape[0], 2):
        pair = jnp.concatenate([x[k], x[k + 1]], axis=1)
        high, low = halves(pair)
        out = fast_dot(mix3, jnp.concatenate([high, low, high], axis=0))
        parts += [out[:, :BL], out[:, BL:]]
    return 0.5 * jnp.tanh(jnp.stack(parts))


def prepare_mixing(mixing_ref, mix3_ref):
    s = mixing_ref.shape[0]
    rows = lax.broadcasted_iota(jnp.int32, (s, s), 0)
    cols = lax.broadcasted_iota(jnp.int32, (s, s), 1)
    flipped = dot(mixing_ref[...], (rows == cols).astype(jnp.float32), TN)
    high, low = halves(flipped)
    mix3_ref[...] = jnp.concatenate([high, high, low], axis=1)


def edge_of(x_ref, f_ref, v_ref, mix3):
    outflow = f_ref[:, :BL][None] * x_ref[:, :, :BL]
    arriving = select(outflow, selector(v_ref[:, :BL], 2 * BL))[:, :, BL:]
    table = selector(v_ref[:, BL:], 2 * BL)
    x = x_ref[:, :, BL:]
    f = f_ref[:, BL:][None]
    outflow = f * x
    routed = select(outflow, table)
    x = x - outflow + (routed[:, :, :BL] + arriving) + blend(x, mix3)
    return routed[:, :, BL:], select(f * x, table)[:, :, BL:]


def edge_kernel(x_ref, f_ref, v_ref, mixing_ref, carry_ref, mix3_ref):
    prepare_mixing(mixing_ref, mix3_ref)
    carry_ref[0], carry_ref[1] = edge_of(x_ref, f_ref, v_ref, mix3_ref[...])


def edge_carries(ensemble, fraction, positions, mixing):
    m, s, r = ensemble.shape
    pair = r // (2 * BL) - 1
    return pl.pallas_call(
        edge_kernel,
        grid=(1,),
        in_specs=[
            pl.BlockSpec((m, s, 2 * BL), lambda g: (0, 0, pair)),
            pl.BlockSpec((s, 2 * BL), lambda g: (0, pair)),
            pl.BlockSpec((1, 2 * BL), lambda g: (0, pair)),
            pl.BlockSpec((s, s), lambda g: (0, 0)),
        ],
        out_specs=pl.BlockSpec((2, m, s, BL), lambda g: (0, 0, 0, 0)),
        out_shape=jax.ShapeDtypeStruct((2, m, s, BL), jnp.float32),
        scratch_shapes=[pltpu.VMEM((s, 3 * s), jnp.bfloat16)],
        compiler_params=pltpu.CompilerParams(vmem_limit_bytes=VMEM_LIMIT),
        name="edge",
    )(ensemble, fraction, positions, mixing)


def forecast_step(x_ref, f_ref, v_ref, slot_ref, out_ref, pack_ref, mix3_ref, carry_ref, block):
    table = selector(v_ref[...], 2 * BL)
    f = f_ref[...][None]
    x = x_ref[...]
    for step in range(2):
        outflow = f * x
        routed = select(outflow, table)
        x = x - outflow + (routed[:, :, :BL] + carry_ref[step]) + blend(x, mix3_ref[...])
        carry_ref[step] = routed[:, :, BL:]
    out_ref[...] = x[None]
    slots = slot_ref[pl.ds(block, 1), :]
    m, s, _ = x.shape
    state_of = slots // BL
    looked = select(x, selector_columns(slots - state_of * BL))
    rows = lax.broadcasted_iota(jnp.int32, (s, slots.shape[1]), 0)
    hot_state = (rows == state_of).astype(jnp.float32)
    seen = jnp.sum(looked * hot_state[None], axis=1)
    mean = jnp.sum(seen, axis=0, keepdims=True) * (1.0 / m)
    pert = seen - mean
    moment = jnp.sum(pert * pert, axis=0, keepdims=True)
    blocks = pack_ref.shape[0]
    pack_ref[pl.ds(block, 1), :m, :] = seen[None]
    pack_ref[:, pl.ds(m + block, 1), :] = jnp.broadcast_to(mean[None], (blocks,) + mean.shape)
    pack_ref[:, pl.ds(m + blocks + block, 1), :] = jnp.broadcast_to(moment[None], (blocks,) + mean.shape)


def inner_kernel(
    x2_ref, f2_ref, v2_ref, x_ref, f_ref, v_ref, mixing_ref, slot_ref, out_ref, pack_ref, mix3_ref, carry_ref
):
    step = pl.program_id(0)

    @pl.when(step == 0)
    def _():
        prepare_mixing(mixing_ref, mix3_ref)
        carry_ref[0], carry_ref[1] = edge_of(x2_ref, f2_ref, v2_ref, mix3_ref[...])

    forecast_step(x_ref, f_ref, v_ref, slot_ref, out_ref, pack_ref, mix3_ref, carry_ref, step + 2)


def outer_kernel(
    halo_ref, pack_in, held_ref, x_ref, f_ref, v_ref, mixing_ref, slot_ref, out_ref, pack_ref, mix3_ref, carry_ref
):
    step = pl.program_id(0)

    @pl.when(step == 0)
    def _():
        prepare_mixing(mixing_ref, mix3_ref)
        carry_ref[...] = halo_ref[...]
        pack_ref[...] = pack_in[...]

    forecast_step(x_ref, f_ref, v_ref, slot_ref, out_ref, pack_ref, mix3_ref, carry_ref, step)


def selector_columns(reach_row):
    slots = reach_row.shape[1]
    rows = lax.broadcasted_iota(jnp.int32, (BL, slots), 0)
    hot = (rows == reach_row).astype(jnp.float32)
    hot = hot.T.astype(jnp.bfloat16)
    return jnp.concatenate([hot, hot], axis=1)


def forecast_blocks(kernel, first, number, lead, lead_specs, ensemble, fraction, positions, mixing, slots, aliases):
    m, s, r = ensemble.shape
    blocks, cap = slots.shape
    whole = lambda *shape: pl.BlockSpec(shape, lambda g: (0,) * len(shape))
    pack = (blocks, m + 2 * blocks, cap)
    return pl.pallas_call(
        kernel,
        grid=(number,),
        in_specs=lead_specs
        + [
            pl.BlockSpec((m, s, BL), lambda g: (0, 0, g + first)),
            pl.BlockSpec((s, BL), lambda g: (0, g + first)),
            pl.BlockSpec((1, BL), lambda g: (0, g + first)),
            whole(s, s),
            whole(blocks, cap),
        ],
        out_specs=[pl.BlockSpec((1, m, s, BL), lambda g: (g + first, 0, 0, 0)), whole(*pack)],
        out_shape=[
            jax.ShapeDtypeStruct((blocks, m, s, BL), jnp.float32),
            jax.ShapeDtypeStruct(pack, jnp.float32),
        ],
        scratch_shapes=[
            pltpu.VMEM((s, 3 * s), jnp.bfloat16),
            pltpu.VMEM((2, m, s, BL), jnp.float32),
        ],
        input_output_aliases=aliases,
        compiler_params=pltpu.CompilerParams(vmem_limit_bytes=VMEM_LIMIT),
        name=kernel.__name__,
    )(*lead, ensemble, fraction, positions, mixing, slots)


def forecast(ensemble, fraction, positions, mixing, slots, halo):
    m, s, r = ensemble.shape
    blocks, cap = slots.shape
    whole = lambda *shape: pl.BlockSpec(shape, lambda g: (0,) * len(shape))
    rest = (ensemble, fraction, positions, mixing, slots)
    out, pack = forecast_blocks(
        inner_kernel, 2, blocks - 2, (ensemble, fraction, positions),
        [whole(m, s, 2 * BL), whole(s, 2 * BL), whole(1, 2 * BL)], *rest, {},
    )
    return forecast_blocks(
        outer_kernel, 0, 2, (halo, pack, out),
        [whole(2, m, s, BL), whole(*pack.shape), pl.BlockSpec(memory_space=pl.ANY)], *rest, {2: 0},
    )


def innovation_kernel(
    block_ref, own_count_ref, pack_ref, values_ref, errors_ref, count_ref, gram_ref, right_ref, sums_ref
):
    blocks, cap = values_ref.shape
    sources = pack_ref.shape[0]
    m = pack_ref.shape[1] - 2 * blocks
    runs = sources * m
    means = pack_ref[:, m : m + blocks, :]
    mean = jnp.sum(means, axis=0) * (1.0 / sources)
    drift = means - mean[None]
    moment = jnp.sum(pack_ref[:, m + blocks :, :], axis=0) + m * jnp.sum(drift * drift, axis=0)
    spread = moment / (runs - 1)
    lanes = lax.broadcasted_iota(jnp.int32, (blocks, cap), 1)
    live = (lanes < count_ref[...]).astype(jnp.float32)
    departure = values_ref[...] - mean
    errors = errors_ref[...]
    terms = live * departure * departure / (errors * errors + spread)
    statistic = jnp.sum(jnp.sum(terms, axis=0, keepdims=True), axis=1, keepdims=True)
    total = jnp.sum(count_ref[...].astype(jnp.float32), axis=0, keepdims=True)
    lanes = lax.broadcasted_iota(jnp.int32, sums_ref.shape, 1)
    sums_ref[...] = jnp.where(lanes < 64, statistic, total)

    own = block_ref[0]
    seen = pack_ref[:, :m, :].reshape(runs, cap)
    mean = jnp.sum(seen, axis=0, keepdims=True) * (1.0 / runs)
    pert = seen - mean
    errors = errors_ref[pl.ds(own, 1), :]
    lanes = lax.broadcasted_iota(jnp.int32, (1, cap), 1)
    live = (lanes < own_count_ref[own]).astype(jnp.float32)
    weighted = pert * (live / (errors * errors))
    departure = values_ref[pl.ds(own, 1), :] - mean
    gram_ref[...] = dot(weighted, pert, NT)
    right_ref[...] = dot(jnp.broadcast_to(departure, (8, cap)), weighted, NT)


def innovations(block, pack, values, errors, counts):
    blocks = values.shape[0]
    runs = pack.shape[0] * (pack.shape[1] - 2 * blocks)
    vmem = pl.BlockSpec(memory_space=pltpu.VMEM)
    smem = pl.BlockSpec(memory_space=pltpu.SMEM)
    return pl.pallas_call(
        innovation_kernel,
        in_specs=[smem, smem, vmem, vmem, vmem, vmem],
        out_specs=[vmem] * 3,
        out_shape=[
            jax.ShapeDtypeStruct((runs, runs), jnp.float32),
            jax.ShapeDtypeStruct((8, runs), jnp.float32),
            jax.ShapeDtypeStruct((8, 128), jnp.float32),
        ],
        name="innovation",
    )(block, counts, pack, values, errors, counts.reshape(blocks, 1))


def small_inverse_factor(a):
    n = a.shape[0]
    rows = lax.broadcasted_iota(jnp.int32, (n, n), 0)
    cols = lax.broadcasted_iota(jnp.int32, (n, n), 1)
    eye = (rows == cols).astype(jnp.float32)
    both = jnp.concatenate([a, eye], axis=1)
    below = lax.broadcasted_iota(jnp.int32, (n, 1), 0)
    scales = jnp.zeros((n, 1), jnp.float32)
    for j in range(n):
        pivot = both[j : j + 1, j : j + 1]
        row = both[j : j + 1, :] * (1.0 / pivot)
        factor = jnp.where(below > j, both[:, j : j + 1], 0.0)
        scales = jnp.where(below == j, pivot, scales)
        both = both - factor * row
    return both[:, n:] * (1.0 / jnp.sqrt(scales))


def inverse_factor(a):
    n = a.shape[0]
    if n <= 32:
        return small_inverse_factor(a)
    h = n // 2
    first = inverse_factor(a[:h, :h])
    cross = dot(a[h:, :h], first, NT)
    second = inverse_factor(a[h:, h:] - dot(cross, cross, NT))
    lower = -dot(second, dot(cross, first))
    zero = jnp.zeros((h, h), jnp.float32)
    return jnp.concatenate(
        [jnp.concatenate([first, zero], axis=1), jnp.concatenate([lower, second], axis=1)], axis=0
    )


def mixer_kernel(gram_ref, right_ref, sums_ref, mixer_ref):
    runs = gram_ref.shape[0]
    inflation = 0.5 + sums_ref[0:1, 0:1] / sums_ref[0:1, 64:65]
    rows = lax.broadcasted_iota(jnp.int32, (runs, runs), 0)
    cols = lax.broadcasted_iota(jnp.int32, (runs, runs), 1)
    system = gram_ref[...] + jnp.where(rows == cols, (runs - 1) / inflation, 0.0)
    inverse = inverse_factor(system)
    half_way = dot(right_ref[...], inverse, NT)
    mean_weight = dot(half_way, inverse)
    mixer_ref[...] = mean_weight[0:1] + jnp.sqrt(jnp.float32(runs - 1)) * inverse


def mixer_of(gram, right, sums):
    vmem = pl.BlockSpec(memory_space=pltpu.VMEM)
    return pl.pallas_call(
        mixer_kernel,
        in_specs=[vmem] * 3,
        out_specs=vmem,
        out_shape=jax.ShapeDtypeStruct(gram.shape, jnp.float32),
        compiler_params=pltpu.CompilerParams(vmem_limit_bytes=VMEM_LIMIT),
        name="mixer",
    )(gram, right, sums)


def apply_kernel(mixer_ref, x_ref, out_ref):
    runs, states, lanes = x_ref.shape
    high, low = halves(mixer_ref[...])
    wide = jnp.concatenate([high, low, high], axis=1)
    x_rows = x_ref.reshape(runs * states, lanes)
    out_rows = out_ref.reshape(runs * states, lanes)
    for s in range(0, states, 2):
        x = jnp.concatenate(
            [x_rows[pl.ds(s + i, runs, stride=states), :] for i in range(2)], axis=1
        )
        mean = jnp.sum(x, axis=0, keepdims=True) * (1.0 / runs)
        x_high, x_low = halves(x - mean)
        out = mean + fast_dot(wide, jnp.concatenate([x_high, x_high, x_low], axis=0))
        for i in range(2):
            out_rows[pl.ds(s + i, runs, stride=states), :] = out[:, i * lanes : (i + 1) * lanes]


def apply_mixer(mixer, x):
    runs, states, lanes = x.shape
    chunk = 8
    block = pl.BlockSpec((runs, chunk, lanes), lambda g: (0, g, 0))
    return pl.pallas_call(
        apply_kernel,
        grid=(states // chunk,),
        in_specs=[pl.BlockSpec((runs, runs), lambda g: (0, 0)), block],
        out_specs=block,
        out_shape=jax.ShapeDtypeStruct(x.shape, jnp.float32),
        compiler_params=pltpu.CompilerParams(vmem_limit_bytes=VMEM_LIMIT),
        name="apply",
    )(mixer, x)


def butterfly_sum(x, axes):
    for axis in axes:
        size = lax.axis_size(axis)
        step = 1
        while step < size:
            x = x + lax.ppermute(x, axis, [(i, i ^ step) for i in range(size)])
            step *= 2
    return x


def on_device(
    ensemble,
    outgoing_fraction,
    mixing,
    downstream_position,
    obs_index,
    obs_value,
    obs_error,
    obs_count,
):
    m, s, r = ensemble.shape
    blocks = r // BL
    reaches = lax.axis_size("reach")
    block = lax.axis_index("mem").astype(jnp.int32).reshape(1)
    routing = (ensemble, outgoing_fraction, downstream_position.reshape(1, r), mixing)
    halo = lax.ppermute(edge_carries(*routing), "reach", [(i, i + 1) for i in range(reaches - 1)])
    prior, pack = forecast(*routing, obs_index, halo)

    pack = lax.all_to_all(pack, "mem", split_axis=0, concat_axis=0, tiled=True)
    gathered = lax.all_to_all(prior, "mem", split_axis=0, concat_axis=0, tiled=True)
    gram, right, sums = innovations(block, pack, obs_value, obs_error, obs_count)
    sums = butterfly_sum(sums, ("reach",))
    mixer = mixer_of(gram, right, sums)
    updated = apply_mixer(mixer, gathered.reshape(blocks * m, s, BL))
    returned = lax.all_to_all(
        updated.reshape(blocks, m, s, BL), "mem", split_axis=0, concat_axis=0, tiled=True
    )
    return jnp.transpose(returned, (1, 2, 0, 3)).reshape(m, s, r)


def solution(mesh):
    placed = (
        P("mem", None, "reach"),
        P(None, "reach"),
        P(),
        P("reach"),
        P("reach", None),
        P("reach", None),
        P("reach", None),
        P("reach"),
    )
    return jax.shard_map(
        on_device, mesh=mesh, in_specs=placed, out_specs=P("mem", None, "reach"), check_vma=False
    )
```

```python
import jax
import jax.numpy as jnp
from jax import lax
from jax.experimental import pallas as pl
from jax.experimental.pallas import tpu as pltpu
from jax.sharding import PartitionSpec as P

BL = 128
HIGHEST = lax.Precision.HIGHEST
NT = (((1,), (1,)), ((), ()))
NN = (((1,), (0,)), ((), ()))
TN = (((0,), (0,)), ((), ()))
VMEM_LIMIT = 48 * 1024 * 1024


def dot(a, b, dims=NN):
    return lax.dot_general(a, b, dims, precision=HIGHEST, preferred_element_type=jnp.float32)


def fast_dot(a, b, dims=NN):
    return lax.dot_general(a, b, dims, preferred_element_type=jnp.float32)


def halves(x):
    high = x.astype(jnp.bfloat16)
    low = (x - high.astype(jnp.float32)).astype(jnp.bfloat16)
    return high, low


def selector(index_row, size):
    rows = lax.broadcasted_iota(jnp.int32, (size, index_row.shape[1]), 0)
    hot = (rows == index_row).astype(jnp.float32).astype(jnp.bfloat16)
    return jnp.concatenate([hot, hot], axis=1)


def select(x, table):
    m, s, r = x.shape
    high, low = halves(x.reshape(m * s, r))
    out = fast_dot(jnp.concatenate([high, low], axis=1), table, NT)
    return out.reshape(m, s, table.shape[0])


def blend(x, mix3):
    parts = []
    for k in range(0, x.shape[0], 2):
        pair = jnp.concatenate([x[k], x[k + 1]], axis=1)
        high, low = halves(pair)
        out = fast_dot(mix3, jnp.concatenate([high, low, high], axis=0))
        parts += [out[:, :BL], out[:, BL:]]
    return 0.5 * jnp.tanh(jnp.stack(parts))


def prepare_mixing(mixing_ref, mix3_ref):
    s = mixing_ref.shape[0]
    rows = lax.broadcasted_iota(jnp.int32, (s, s), 0)
    cols = lax.broadcasted_iota(jnp.int32, (s, s), 1)
    flipped = dot(mixing_ref[...], (rows == cols).astype(jnp.float32), TN)
    high, low = halves(flipped)
    mix3_ref[...] = jnp.concatenate([high, high, low], axis=1)


def edge_of(x_ref, f_ref, v_ref, mix3):
    outflow = f_ref[:, :BL][None] * x_ref[:, :, :BL]
    arriving = select(outflow, selector(v_ref[:, :BL], 2 * BL))[:, :, BL:]
    table = selector(v_ref[:, BL:], 2 * BL)
    x = x_ref[:, :, BL:]
    f = f_ref[:, BL:][None]
    outflow = f * x
    routed = select(outflow, table)
    x = x - outflow + (routed[:, :, :BL] + arriving) + blend(x, mix3)
    return routed[:, :, BL:], select(f * x, table)[:, :, BL:]


def edge_kernel(x_ref, f_ref, v_ref, mixing_ref, carry_ref, mix3_ref):
    prepare_mixing(mixing_ref, mix3_ref)
    carry_ref[0], carry_ref[1] = edge_of(x_ref, f_ref, v_ref, mix3_ref[...])


def edge_carries(ensemble, fraction, positions, mixing):
    m, s, r = ensemble.shape
    pair = r // (2 * BL) - 1
    return pl.pallas_call(
        edge_kernel,
        grid=(1,),
        in_specs=[
            pl.BlockSpec((m, s, 2 * BL), lambda g: (0, 0, pair)),
            pl.BlockSpec((s, 2 * BL), lambda g: (0, pair)),
            pl.BlockSpec((1, 2 * BL), lambda g: (0, pair)),
            pl.BlockSpec((s, s), lambda g: (0, 0)),
        ],
        out_specs=pl.BlockSpec((2, m, s, BL), lambda g: (0, 0, 0, 0)),
        out_shape=jax.ShapeDtypeStruct((2, m, s, BL), jnp.float32),
        scratch_shapes=[pltpu.VMEM((s, 3 * s), jnp.bfloat16)],
        compiler_params=pltpu.CompilerParams(vmem_limit_bytes=VMEM_LIMIT),
        name="edge",
    )(ensemble, fraction, positions, mixing)


def forecast_step(x, f, v, slots, mix3, carry_ref):
    m, s, _ = x.shape
    table = selector(v, 2 * BL)
    f = f[None]
    for step in range(2):
        outflow = f * x
        routed = select(outflow, table)
        x = x - outflow + (routed[:, :, :BL] + carry_ref[step]) + blend(x, mix3)
        carry_ref[step] = routed[:, :, BL:]
    state_of = slots // BL
    looked = select(x, selector_columns(slots - state_of * BL))
    rows = lax.broadcasted_iota(jnp.int32, (s, slots.shape[1]), 0)
    hot_state = (rows == state_of).astype(jnp.float32)
    seen = jnp.sum(looked * hot_state[None], axis=1)
    mean = jnp.sum(seen, axis=0, keepdims=True) * (1.0 / m)
    pert = seen - mean
    return x, seen, mean, jnp.sum(pert * pert, axis=0, keepdims=True)


def store_block(x, seen, near_ref, far_ref, at):
    m, s, lanes = x.shape
    rows = m // 2 * s
    near_ref[at, :rows, :] = x[: m // 2].reshape(rows, lanes)
    far_ref[at] = x[m // 2 :].reshape(rows, lanes)
    near_ref[at, rows : rows + m, :] = seen[:, :BL]
    near_ref[at, rows + m : rows + 2 * m, :] = seen[:, BL:]


def store_moments(mean, moment, moments_ref, block):
    blocks = moments_ref.shape[0] // 4
    for k, part in enumerate((mean[:, :BL], mean[:, BL:], moment[:, :BL], moment[:, BL:])):
        moments_ref[pl.ds(k * blocks + block, 1), :] = part


def inner_kernel(
    x2_ref, f2_ref, v2_ref, x_ref, f_ref, v_ref, mixing_ref, slot_ref,
    near_ref, far_ref, moments_ref, mix3_ref, carry_ref,
):
    step = pl.program_id(0)

    @pl.when(step == 0)
    def _():
        prepare_mixing(mixing_ref, mix3_ref)
        carry_ref[0], carry_ref[1] = edge_of(x2_ref, f2_ref, v2_ref, mix3_ref[...])

    block = step + 2
    x, seen, mean, moment = forecast_step(
        x_ref[...], f_ref[...], v_ref[...], slot_ref[pl.ds(block, 1), :], mix3_ref[...], carry_ref
    )
    store_block(x, seen, near_ref, far_ref, 0)
    store_moments(mean, moment, moments_ref, block)


def outer_kernel(
    x_ref, f_ref, v_ref, mixing_ref, slot_ref, halo_ref, moments_in, near_in, far_in,
    near_ref, far_ref, mix3_ref, carry_ref, near_buffer, far_buffer, moments_buffer, spread_buffer, sems,
):
    blocks = near_ref.shape[0]
    prepare_mixing(mixing_ref, mix3_ref)
    carry_ref[...] = halo_ref[...]
    moments_buffer[...] = moments_in[...]
    for block in range(2):
        lanes = slice(block * BL, (block + 1) * BL)
        x, seen, mean, moment = forecast_step(
            x_ref[:, :, lanes], f_ref[:, lanes], v_ref[:, lanes], slot_ref[block : block + 1, :],
            mix3_ref[...], carry_ref,
        )
        store_block(x, seen, near_buffer, far_buffer, block)
        store_moments(mean, moment, moments_buffer, block)
    first = near_buffer.shape[1] - moments_buffer.shape[0]
    moments = moments_buffer[...]
    near_buffer[:, first:, :] = jnp.broadcast_to(moments[None], (2,) + moments.shape)
    spread_buffer[...] = jnp.broadcast_to(moments[None], spread_buffer.shape)
    copies = [
        pltpu.make_async_copy(near_buffer, near_ref.at[0:2], sems.at[0]),
        pltpu.make_async_copy(far_buffer, far_ref.at[0:2], sems.at[1]),
        pltpu.make_async_copy(
            spread_buffer, near_ref.at[2:blocks, first : first + moments.shape[0], :], sems.at[2]
        ),
    ]
    for copy in copies:
        copy.start()
    for copy in copies:
        copy.wait()


def selector_columns(reach_row):
    slots = reach_row.shape[1]
    rows = lax.broadcasted_iota(jnp.int32, (BL, slots), 0)
    hot = (rows == reach_row).astype(jnp.float32)
    hot = hot.T.astype(jnp.bfloat16)
    return jnp.concatenate([hot, hot], axis=1)


def forecast(ensemble, fraction, positions, mixing, slots, halo):
    m, s, r = ensemble.shape
    blocks, cap = slots.shape
    whole = lambda *shape: pl.BlockSpec(shape, lambda g: (0,) * len(shape))
    held = pl.BlockSpec(memory_space=pl.ANY)
    pair = [whole(m, s, 2 * BL), whole(s, 2 * BL), whole(1, 2 * BL)]
    rows = m // 2 * s
    extra = 2 * m + 4 * blocks
    near = jax.ShapeDtypeStruct((blocks, rows + extra, BL), jnp.float32)
    far = jax.ShapeDtypeStruct((blocks, rows, BL), jnp.float32)
    mix3 = pltpu.VMEM((s, 3 * s), jnp.bfloat16)
    carry = pltpu.VMEM((2, m, s, BL), jnp.float32)
    routing = (ensemble, fraction, positions)
    near_part, far_part, moments = pl.pallas_call(
        inner_kernel,
        grid=(blocks - 2,),
        in_specs=pair
        + [
            pl.BlockSpec((m, s, BL), lambda g: (0, 0, g + 2)),
            pl.BlockSpec((s, BL), lambda g: (0, g + 2)),
            pl.BlockSpec((1, BL), lambda g: (0, g + 2)),
            whole(s, s),
            whole(blocks, cap),
        ],
        out_specs=[
            pl.BlockSpec((1, rows + extra, BL), lambda g: (g + 2, 0, 0)),
            pl.BlockSpec((1, rows, BL), lambda g: (g + 2, 0, 0)),
            whole(4 * blocks, BL),
        ],
        out_shape=[near, far, jax.ShapeDtypeStruct((4 * blocks, BL), jnp.float32)],
        scratch_shapes=[mix3, carry],
        compiler_params=pltpu.CompilerParams(vmem_limit_bytes=VMEM_LIMIT),
        name="inner",
    )(*routing, *routing, mixing, slots)
    return pl.pallas_call(
        outer_kernel,
        grid=(1,),
        in_specs=pair + [whole(s, s), whole(blocks, cap), whole(2, m, s, BL), whole(4 * blocks, BL), held, held],
        out_specs=[held, held],
        out_shape=[near, far],
        scratch_shapes=[
            mix3,
            carry,
            pltpu.VMEM((2,) + near.shape[1:], jnp.float32),
            pltpu.VMEM((2,) + far.shape[1:], jnp.float32),
            pltpu.VMEM((4 * blocks, BL), jnp.float32),
            pltpu.VMEM((blocks - 2, 4 * blocks, BL), jnp.float32),
            pltpu.SemaphoreType.DMA((3,)),
        ],
        input_output_aliases={7: 0, 8: 1},
        compiler_params=pltpu.CompilerParams(vmem_limit_bytes=VMEM_LIMIT),
        name="outer",
    )(*routing, mixing, slots, halo, moments, near_part, far_part)


def innovation_kernel(
    block_ref, own_count_ref, near_ref, values_ref, errors_ref, count_ref, gram_ref, right_ref, sums_ref
):
    blocks, cap = values_ref.shape
    sources = near_ref.shape[0]
    m = (near_ref.shape[1] - 4 * blocks) // 2
    runs = sources * m
    joined = lambda at, size: jnp.concatenate(
        [near_ref[:, at : at + size, :], near_ref[:, at + size : at + 2 * size, :]], axis=2
    )
    means = joined(2 * m, blocks)
    mean = jnp.sum(means, axis=0) * (1.0 / sources)
    drift = means - mean[None]
    moment = jnp.sum(joined(2 * m + 2 * blocks, blocks), axis=0) + m * jnp.sum(drift * drift, axis=0)
    spread = moment / (runs - 1)
    lanes = lax.broadcasted_iota(jnp.int32, (blocks, cap), 1)
    live = (lanes < count_ref[...]).astype(jnp.float32)
    departure = values_ref[...] - mean
    errors = errors_ref[...]
    terms = live * departure * departure / (errors * errors + spread)
    statistic = jnp.sum(jnp.sum(terms, axis=0, keepdims=True), axis=1, keepdims=True)
    total = jnp.sum(count_ref[...].astype(jnp.float32), axis=0, keepdims=True)
    lanes = lax.broadcasted_iota(jnp.int32, sums_ref.shape, 1)
    sums_ref[...] = jnp.where(lanes < 64, statistic, total)

    own = block_ref[0]
    seen = joined(0, m).reshape(runs, cap)
    mean = jnp.sum(seen, axis=0, keepdims=True) * (1.0 / runs)
    pert = seen - mean
    errors = errors_ref[pl.ds(own, 1), :]
    lanes = lax.broadcasted_iota(jnp.int32, (1, cap), 1)
    live = (lanes < own_count_ref[own]).astype(jnp.float32)
    weighted = pert * (live / (errors * errors))
    departure = values_ref[pl.ds(own, 1), :] - mean
    gram_ref[...] = dot(weighted, pert, NT)
    right_ref[...] = dot(jnp.broadcast_to(departure, (8, cap)), weighted, NT)


def innovations(block, near, values, errors, counts, m):
    blocks, cap = values.shape
    sources, rows, lanes = near.shape
    extra = 2 * m + 4 * blocks
    runs = sources * m
    whole = lambda *shape: pl.BlockSpec(shape, lambda g: (0,) * len(shape))
    smem = pl.BlockSpec(memory_space=pltpu.SMEM)
    return pl.pallas_call(
        innovation_kernel,
        grid=(1,),
        in_specs=[
            smem,
            smem,
            pl.BlockSpec((sources, extra, lanes), lambda g: (0, rows // extra - 1, 0)),
            whole(blocks, cap),
            whole(blocks, cap),
            whole(blocks, 1),
        ],
        out_specs=[whole(runs, runs), whole(8, runs), whole(8, 128)],
        out_shape=[
            jax.ShapeDtypeStruct((runs, runs), jnp.float32),
            jax.ShapeDtypeStruct((8, runs), jnp.float32),
            jax.ShapeDtypeStruct((8, 128), jnp.float32),
        ],
        name="innovation",
    )(block, counts, near, values, errors, counts.reshape(blocks, 1))


def small_inverse_factor(a):
    n = a.shape[0]
    rows = lax.broadcasted_iota(jnp.int32, (n, n), 0)
    cols = lax.broadcasted_iota(jnp.int32, (n, n), 1)
    eye = (rows == cols).astype(jnp.float32)
    both = jnp.concatenate([a, eye], axis=1)
    below = lax.broadcasted_iota(jnp.int32, (n, 1), 0)
    scales = jnp.zeros((n, 1), jnp.float32)
    for j in range(n):
        pivot = both[j : j + 1, j : j + 1]
        row = both[j : j + 1, :] * (1.0 / pivot)
        factor = jnp.where(below > j, both[:, j : j + 1], 0.0)
        scales = jnp.where(below == j, pivot, scales)
        both = both - factor * row
    return both[:, n:] * (1.0 / jnp.sqrt(scales))


def inverse_factor(a):
    n = a.shape[0]
    if n <= 32:
        return small_inverse_factor(a)
    h = n // 2
    first = inverse_factor(a[:h, :h])
    cross = dot(a[h:, :h], first, NT)
    second = inverse_factor(a[h:, h:] - dot(cross, cross, NT))
    lower = -dot(second, dot(cross, first))
    zero = jnp.zeros((h, h), jnp.float32)
    return jnp.concatenate(
        [jnp.concatenate([first, zero], axis=1), jnp.concatenate([lower, second], axis=1)], axis=0
    )


def mixer_kernel(gram_ref, right_ref, sums_ref, mixer_ref):
    runs = gram_ref.shape[0]
    inflation = 0.5 + sums_ref[0:1, 0:1] / sums_ref[0:1, 64:65]
    rows = lax.broadcasted_iota(jnp.int32, (runs, runs), 0)
    cols = lax.broadcasted_iota(jnp.int32, (runs, runs), 1)
    system = gram_ref[...] + jnp.where(rows == cols, (runs - 1) / inflation, 0.0)
    inverse = inverse_factor(system)
    half_way = dot(right_ref[...], inverse, NT)
    mean_weight = dot(half_way, inverse)
    mixer_ref[...] = mean_weight[0:1] + jnp.sqrt(jnp.float32(runs - 1)) * inverse


def mixer_of(gram, right, sums):
    vmem = pl.BlockSpec(memory_space=pltpu.VMEM)
    return pl.pallas_call(
        mixer_kernel,
        in_specs=[vmem] * 3,
        out_specs=vmem,
        out_shape=jax.ShapeDtypeStruct(gram.shape, jnp.float32),
        compiler_params=pltpu.CompilerParams(vmem_limit_bytes=VMEM_LIMIT),
        name="mixer",
    )(gram, right, sums)


def apply_kernel(mixer_ref, near_ref, far_ref, out_ref):
    sources, half, states, lanes = near_ref.shape
    runs = 2 * sources * half
    high, low = halves(mixer_ref[...])
    wide = jnp.concatenate([high, low, high], axis=1)
    flat = lambda ref: ref.reshape(sources * half * states, lanes)
    near_rows, far_rows = flat(near_ref), flat(far_ref)
    out_rows = out_ref.reshape(runs * states, lanes)

    def members(s):
        parts = [
            rows[pl.ds(s, sources * half, stride=states), :].reshape(sources, half, lanes)
            for rows in (near_rows, far_rows)
        ]
        return jnp.concatenate(parts, axis=1).reshape(runs, lanes)

    for s in range(0, states, 2):
        x = jnp.concatenate([members(s), members(s + 1)], axis=1)
        mean = jnp.sum(x, axis=0, keepdims=True) * (1.0 / runs)
        x_high, x_low = halves(x - mean)
        out = mean + fast_dot(wide, jnp.concatenate([x_high, x_high, x_low], axis=0))
        for i in range(2):
            out_rows[pl.ds(s + i, runs, stride=states), :] = out[:, i * lanes : (i + 1) * lanes]


def apply_mixer(mixer, near, far, chunk=8):
    sources, half, states, lanes = far.shape
    runs = 2 * sources * half
    part = pl.BlockSpec((sources, half, chunk, lanes), lambda g: (0, 0, g, 0))
    return pl.pallas_call(
        apply_kernel,
        grid=(states // chunk,),
        in_specs=[pl.BlockSpec((runs, runs), lambda g: (0, 0)), part, part],
        out_specs=pl.BlockSpec((runs, chunk, lanes), lambda g: (0, g, 0)),
        out_shape=jax.ShapeDtypeStruct((runs, states, lanes), jnp.float32),
        compiler_params=pltpu.CompilerParams(vmem_limit_bytes=VMEM_LIMIT),
        name="apply",
    )(mixer, near, far)


def butterfly_sum(x, axes):
    for axis in axes:
        size = lax.axis_size(axis)
        step = 1
        while step < size:
            x = x + lax.ppermute(x, axis, [(i, i ^ step) for i in range(size)])
            step *= 2
    return x


def on_device(
    ensemble,
    outgoing_fraction,
    mixing,
    downstream_position,
    obs_index,
    obs_value,
    obs_error,
    obs_count,
):
    m, s, r = ensemble.shape
    blocks = r // BL
    reaches = lax.axis_size("reach")
    block = lax.axis_index("mem").astype(jnp.int32).reshape(1)
    routing = (ensemble, outgoing_fraction, downstream_position.reshape(1, r), mixing)
    halo = lax.ppermute(edge_carries(*routing), "reach", [(i, i + 1) for i in range(reaches - 1)])
    near, far = forecast(*routing, obs_index, halo)

    near = lax.all_to_all(near, "mem", split_axis=0, concat_axis=0, tiled=True)
    far = lax.all_to_all(far, "mem", split_axis=0, concat_axis=0, tiled=True)
    gram, right, sums = innovations(block, near, obs_value, obs_error, obs_count, m)
    sums = butterfly_sum(sums, ("reach",))
    mixer = mixer_of(gram, right, sums)
    updated = apply_mixer(mixer, near.reshape(blocks, -1, s, BL), far.reshape(blocks, -1, s, BL))
    returned = lax.all_to_all(
        updated.reshape(blocks, m, s, BL), "mem", split_axis=0, concat_axis=0, tiled=True
    )
    return jnp.transpose(returned, (1, 2, 0, 3)).reshape(m, s, r)


def solution(mesh):
    placed = (
        P("mem", None, "reach"),
        P(None, "reach"),
        P(),
        P("reach"),
        P("reach", None),
        P("reach", None),
        P("reach", None),
        P("reach"),
    )
    return jax.shard_map(
        on_device, mesh=mesh, in_specs=placed, out_specs=P("mem", None, "reach"), check_vma=False
    )
```

```python
import jax
import jax.numpy as jnp
from jax import lax
from jax.experimental import pallas as pl
from jax.experimental.pallas import tpu as pltpu
from jax.sharding import PartitionSpec as P

BL = 128
HIGHEST = lax.Precision.HIGHEST
NT = (((1,), (1,)), ((), ()))
NN = (((1,), (0,)), ((), ()))
TN = (((0,), (0,)), ((), ()))
VMEM_LIMIT = 24 * 1024 * 1024


def dot(a, b, dims=NN):
    return lax.dot_general(a, b, dims, precision=HIGHEST, preferred_element_type=jnp.float32)


def fast_dot(a, b, dims=NN):
    return lax.dot_general(a, b, dims, preferred_element_type=jnp.float32)


def halves(x):
    high = x.astype(jnp.bfloat16)
    low = (x - high.astype(jnp.float32)).astype(jnp.bfloat16)
    return high, low


def one_hot(index, iota):
    return (index == iota).astype(jnp.float32).astype(jnp.bfloat16)


def target_table(position_row):
    reaches = position_row.shape[1]
    column = jnp.broadcast_to(position_row, (reaches, reaches)).T
    lanes = lax.broadcasted_iota(jnp.int32, (reaches, reaches), 1)
    hot = jnp.concatenate([one_hot(column, lanes), one_hot(column, lanes + reaches)], axis=1)
    return jnp.concatenate([hot, hot], axis=0)


def slot_table(reach_row):
    rows = lax.broadcasted_iota(jnp.int32, (BL, reach_row.shape[1]), 0)
    hot = one_hot(reach_row, rows)
    return jnp.concatenate([hot, hot], axis=0)


def select(x, table):
    m, s, r = x.shape
    high, low = halves(x.reshape(m * s, r))
    out = fast_dot(jnp.concatenate([high, low], axis=1), table)
    return out.reshape(m, s, table.shape[1])


def blend(x, mix3):
    parts = []
    for k in range(0, x.shape[0], 2):
        pair = jnp.concatenate([x[k], x[k + 1]], axis=1)
        high, low = halves(pair)
        out = fast_dot(mix3, jnp.concatenate([high, low, high], axis=0))
        parts += [out[:, :BL], out[:, BL:]]
    return 0.5 * jnp.tanh(jnp.stack(parts))


def prepare_mixing(mixing_ref, mix3_ref):
    s = mixing_ref.shape[0]
    rows = lax.broadcasted_iota(jnp.int32, (s, s), 0)
    cols = lax.broadcasted_iota(jnp.int32, (s, s), 1)
    flipped = dot(mixing_ref[...], (rows == cols).astype(jnp.float32), TN)
    high, low = halves(flipped)
    mix3_ref[...] = jnp.concatenate([high, high, low], axis=1)


def edge_of(x_ref, f_ref, v_ref, mix3):
    outflow = f_ref[:, :BL][None] * x_ref[:, :, :BL]
    arriving = select(outflow, target_table(v_ref[:, :BL]))[:, :, BL:]
    table = target_table(v_ref[:, BL:])
    x = x_ref[:, :, BL:]
    f = f_ref[:, BL:][None]
    outflow = f * x
    routed = select(outflow, table)
    x = x - outflow + (routed[:, :, :BL] + arriving) + blend(x, mix3)
    return routed[:, :, BL:], select(f * x, table)[:, :, BL:]


def edge_kernel(x_ref, f_ref, v_ref, mixing_ref, carry_ref, mix3_ref):
    prepare_mixing(mixing_ref, mix3_ref)
    carry_ref[0], carry_ref[1] = edge_of(x_ref, f_ref, v_ref, mix3_ref[...])


def edge_carries(ensemble, fraction, positions, mixing):
    m, s, r = ensemble.shape
    pair = r // (2 * BL) - 1
    return pl.pallas_call(
        edge_kernel,
        grid=(1,),
        in_specs=[
            pl.BlockSpec((m, s, 2 * BL), lambda g: (0, 0, pair)),
            pl.BlockSpec((s, 2 * BL), lambda g: (0, pair)),
            pl.BlockSpec((1, 2 * BL), lambda g: (0, pair)),
            pl.BlockSpec((s, s), lambda g: (0, 0)),
        ],
        out_specs=pl.BlockSpec((2, m, s, BL), lambda g: (0, 0, 0, 0)),
        out_shape=jax.ShapeDtypeStruct((2, m, s, BL), jnp.float32),
        scratch_shapes=[pltpu.VMEM((s, 3 * s), jnp.bfloat16)],
        compiler_params=pltpu.CompilerParams(vmem_limit_bytes=VMEM_LIMIT),
        name="edge",
    )(ensemble, fraction, positions, mixing)


def forecast_step(x, f, v, slots, mix3, carry_ref):
    m, s, _ = x.shape
    table = target_table(v)
    f = f[None]
    for step in range(2):
        outflow = f * x
        routed = select(outflow, table)
        x = x - outflow + (routed[:, :, :BL] + carry_ref[step]) + blend(x, mix3)
        carry_ref[step] = routed[:, :, BL:]
    state_of = slots // BL
    looked = select(x, slot_table(slots - state_of * BL))
    rows = lax.broadcasted_iota(jnp.int32, (s, slots.shape[1]), 0)
    hot_state = (rows == state_of).astype(jnp.float32)
    seen = jnp.sum(looked * hot_state[None], axis=1)
    mean = jnp.sum(seen, axis=0, keepdims=True) * (1.0 / m)
    pert = seen - mean
    return x, seen, mean, jnp.sum(pert * pert, axis=0, keepdims=True)


def store_block(x, seen, near_ref, far_ref, at):
    m, s, lanes = x.shape
    rows = m // 2 * s
    near_ref[at, :rows, :] = x[: m // 2].reshape(rows, lanes)
    far_ref[at] = x[m // 2 :].reshape(rows, lanes)
    near_ref[at, rows : rows + m, :] = seen[:, :BL]
    near_ref[at, rows + m : rows + 2 * m, :] = seen[:, BL:]


def store_moments(mean, moment, moments_ref, block):
    blocks = moments_ref.shape[0] // 4
    for k, part in enumerate((mean[:, :BL], mean[:, BL:], moment[:, :BL], moment[:, BL:])):
        moments_ref[pl.ds(k * blocks + block, 1), :] = part


def inner_kernel(
    x2_ref, f2_ref, v2_ref, x_ref, f_ref, v_ref, mixing_ref, slot_ref,
    near_ref, far_ref, moments_ref, mix3_ref, carry_ref,
):
    step = pl.program_id(0)

    @pl.when(step == 0)
    def _():
        prepare_mixing(mixing_ref, mix3_ref)
        carry_ref[0], carry_ref[1] = edge_of(x2_ref, f2_ref, v2_ref, mix3_ref[...])

    for i in range(2):
        block = 2 * step + 2 + i
        lanes = slice(i * BL, (i + 1) * BL)
        x, seen, mean, moment = forecast_step(
            x_ref[:, :, lanes], f_ref[:, lanes], v_ref[:, lanes], slot_ref[pl.ds(block, 1), :],
            mix3_ref[...], carry_ref,
        )
        store_block(x, seen, near_ref, far_ref, i)
        store_moments(mean, moment, moments_ref, block)


def outer_kernel(
    x_ref, f_ref, v_ref, mixing_ref, slot_ref, halo_ref, moments_in, near_in, far_in,
    near_ref, far_ref, mix3_ref, carry_ref, near_buffer, far_buffer, moments_buffer, spread_buffer, sems,
):
    blocks = near_ref.shape[0]
    prepare_mixing(mixing_ref, mix3_ref)
    carry_ref[...] = halo_ref[...]
    moments_buffer[...] = moments_in[...]
    for block in range(2):
        lanes = slice(block * BL, (block + 1) * BL)
        x, seen, mean, moment = forecast_step(
            x_ref[:, :, lanes], f_ref[:, lanes], v_ref[:, lanes], slot_ref[block : block + 1, :],
            mix3_ref[...], carry_ref,
        )
        store_block(x, seen, near_buffer, far_buffer, block)
        store_moments(mean, moment, moments_buffer, block)
    first = near_buffer.shape[1] - moments_buffer.shape[0]
    moments = moments_buffer[...]
    near_buffer[:, first:, :] = jnp.broadcast_to(moments[None], (2,) + moments.shape)
    spread_buffer[...] = jnp.broadcast_to(moments[None], spread_buffer.shape)
    copies = [
        pltpu.make_async_copy(near_buffer, near_ref.at[0:2], sems.at[0]),
        pltpu.make_async_copy(far_buffer, far_ref.at[0:2], sems.at[1]),
        pltpu.make_async_copy(
            spread_buffer, near_ref.at[2:blocks, first : first + moments.shape[0], :], sems.at[2]
        ),
    ]
    for copy in copies:
        copy.start()
    for copy in copies:
        copy.wait()


def forecast(ensemble, fraction, positions, mixing, slots, halo):
    m, s, r = ensemble.shape
    blocks, cap = slots.shape
    whole = lambda *shape: pl.BlockSpec(shape, lambda g: (0,) * len(shape))
    held = pl.BlockSpec(memory_space=pl.ANY)
    pair = [whole(m, s, 2 * BL), whole(s, 2 * BL), whole(1, 2 * BL)]
    rows = m // 2 * s
    extra = 2 * m + 4 * blocks
    near = jax.ShapeDtypeStruct((blocks, rows + extra, BL), jnp.float32)
    far = jax.ShapeDtypeStruct((blocks, rows, BL), jnp.float32)
    mix3 = pltpu.VMEM((s, 3 * s), jnp.bfloat16)
    carry = pltpu.VMEM((2, m, s, BL), jnp.float32)
    routing = (ensemble, fraction, positions)
    near_part, far_part, moments = pl.pallas_call(
        inner_kernel,
        grid=(blocks // 2 - 1,),
        in_specs=pair
        + [
            pl.BlockSpec((m, s, 2 * BL), lambda g: (0, 0, g + 1)),
            pl.BlockSpec((s, 2 * BL), lambda g: (0, g + 1)),
            pl.BlockSpec((1, 2 * BL), lambda g: (0, g + 1)),
            whole(s, s),
            whole(blocks, cap),
        ],
        out_specs=[
            pl.BlockSpec((2, rows + extra, BL), lambda g: (g + 1, 0, 0)),
            pl.BlockSpec((2, rows, BL), lambda g: (g + 1, 0, 0)),
            whole(4 * blocks, BL),
        ],
        out_shape=[near, far, jax.ShapeDtypeStruct((4 * blocks, BL), jnp.float32)],
        scratch_shapes=[mix3, carry],
        compiler_params=pltpu.CompilerParams(vmem_limit_bytes=VMEM_LIMIT),
        name="inner",
    )(*routing, *routing, mixing, slots)
    return pl.pallas_call(
        outer_kernel,
        grid=(1,),
        in_specs=pair + [whole(s, s), whole(blocks, cap), whole(2, m, s, BL), whole(4 * blocks, BL), held, held],
        out_specs=[held, held],
        out_shape=[near, far],
        scratch_shapes=[
            mix3,
            carry,
            pltpu.VMEM((2,) + near.shape[1:], jnp.float32),
            pltpu.VMEM((2,) + far.shape[1:], jnp.float32),
            pltpu.VMEM((4 * blocks, BL), jnp.float32),
            pltpu.VMEM((blocks - 2, 4 * blocks, BL), jnp.float32),
            pltpu.SemaphoreType.DMA((3,)),
        ],
        input_output_aliases={7: 0, 8: 1},
        compiler_params=pltpu.CompilerParams(vmem_limit_bytes=VMEM_LIMIT),
        name="outer",
    )(*routing, mixing, slots, halo, moments, near_part, far_part)


def innovation_kernel(
    block_ref, own_count_ref, near_ref, values_ref, errors_ref, count_ref, gram_ref, right_ref, sums_ref
):
    blocks, cap = values_ref.shape
    sources = near_ref.shape[0]
    m = (near_ref.shape[1] - 4 * blocks) // 2
    runs = sources * m
    joined = lambda at, size: jnp.concatenate(
        [near_ref[:, at : at + size, :], near_ref[:, at + size : at + 2 * size, :]], axis=2
    )
    means = joined(2 * m, blocks)
    mean = jnp.sum(means, axis=0) * (1.0 / sources)
    drift = means - mean[None]
    moment = jnp.sum(joined(2 * m + 2 * blocks, blocks), axis=0) + m * jnp.sum(drift * drift, axis=0)
    spread = moment / (runs - 1)
    lanes = lax.broadcasted_iota(jnp.int32, (blocks, cap), 1)
    live = (lanes < count_ref[...]).astype(jnp.float32)
    departure = values_ref[...] - mean
    errors = errors_ref[...]
    terms = live * departure * departure / (errors * errors + spread)
    statistic = jnp.sum(jnp.sum(terms, axis=0, keepdims=True), axis=1, keepdims=True)
    total = jnp.sum(count_ref[...].astype(jnp.float32), axis=0, keepdims=True)
    lanes = lax.broadcasted_iota(jnp.int32, sums_ref.shape, 1)
    sums_ref[...] = jnp.where(lanes < 64, statistic, total)

    own = block_ref[0]
    seen = joined(0, m).reshape(runs, cap)
    mean = jnp.sum(seen, axis=0, keepdims=True) * (1.0 / runs)
    pert = seen - mean
    errors = errors_ref[pl.ds(own, 1), :]
    lanes = lax.broadcasted_iota(jnp.int32, (1, cap), 1)
    live = (lanes < own_count_ref[own]).astype(jnp.float32)
    weighted = pert * (live / (errors * errors))
    departure = values_ref[pl.ds(own, 1), :] - mean
    gram_ref[...] = dot(weighted, pert, NT)
    right_ref[...] = dot(jnp.broadcast_to(departure, (8, cap)), weighted, NT)


def innovations(block, near, values, errors, counts, m):
    blocks, cap = values.shape
    sources, rows, lanes = near.shape
    extra = 2 * m + 4 * blocks
    runs = sources * m
    whole = lambda *shape: pl.BlockSpec(shape, lambda g: (0,) * len(shape))
    smem = pl.BlockSpec(memory_space=pltpu.SMEM)
    return pl.pallas_call(
        innovation_kernel,
        grid=(1,),
        in_specs=[
            smem,
            smem,
            pl.BlockSpec((sources, extra, lanes), lambda g: (0, rows // extra - 1, 0)),
            whole(blocks, cap),
            whole(blocks, cap),
            whole(blocks, 1),
        ],
        out_specs=[whole(runs, runs), whole(8, runs), whole(8, 128)],
        out_shape=[
            jax.ShapeDtypeStruct((runs, runs), jnp.float32),
            jax.ShapeDtypeStruct((8, runs), jnp.float32),
            jax.ShapeDtypeStruct((8, 128), jnp.float32),
        ],
        name="innovation",
    )(block, counts, near, values, errors, counts.reshape(blocks, 1))


def small_inverse_factor(a):
    n = a.shape[0]
    rows = lax.broadcasted_iota(jnp.int32, (n, n), 0)
    cols = lax.broadcasted_iota(jnp.int32, (n, n), 1)
    both = jnp.concatenate([a, (rows == cols).astype(jnp.float32)], axis=1)
    groups = [both[k : k + 8] for k in range(0, n, 8)]
    sub = lax.broadcasted_iota(jnp.int32, (8, 2 * n), 0)
    lane = lambda x, j: jnp.broadcast_to(x[:, j : j + 1], x.shape)
    line = lambda x, i: jnp.broadcast_to(x[i : i + 1], x.shape)
    scales = []
    for j in range(0, n, 2):
        k, i = divmod(j, 8)
        head = groups[k]
        first = [lane(g, j) for g in groups[k:]]
        second = [lane(g, j + 1) for g in groups[k:]]
        p, q, t = line(first[0], i), line(second[0], i), line(second[0], i + 1)
        top, bottom = line(head, i), line(head, i + 1)
        scale_top = 1.0 / p
        scale_bottom = p * (1.0 / (p * t - q * q))
        slope = q * scale_top
        bottom = bottom - slope * top
        bottom_row = bottom * scale_bottom
        top_row = top * scale_top - slope * bottom_row
        groups[k:] = [
            g - f * top_row - h * bottom_row for g, f, h in zip(groups[k:], first, second)
        ]
        groups[k] = jnp.where(sub > i + 1, groups[k], jnp.where(sub == i + 1, bottom, head))
        if i == 0:
            scales.append(scale_top)
        scales[k] = jnp.where(sub > i, scale_bottom, jnp.where(sub == i, scale_top, scales[k]))
    inverse = jnp.concatenate([g * jnp.sqrt(c) for g, c in zip(groups, scales)], axis=0)
    return inverse[:, n:]


def inverse_factor(a):
    n = a.shape[0]
    if n <= 64:
        return small_inverse_factor(a)
    h = n // 2
    first = inverse_factor(a[:h, :h])
    cross = dot(a[h:, :h], first, NT)
    second = inverse_factor(a[h:, h:] - dot(cross, cross, NT))
    lower = -dot(second, dot(cross, first))
    zero = jnp.zeros((h, h), jnp.float32)
    return jnp.concatenate(
        [jnp.concatenate([first, zero], axis=1), jnp.concatenate([lower, second], axis=1)], axis=0
    )


def mixer_kernel(gram_ref, right_ref, sums_ref, mixer_ref):
    runs = gram_ref.shape[0]
    inflation = 0.5 + sums_ref[0:1, 0:1] / sums_ref[0:1, 64:65]
    rows = lax.broadcasted_iota(jnp.int32, (runs, runs), 0)
    cols = lax.broadcasted_iota(jnp.int32, (runs, runs), 1)
    system = gram_ref[...] + jnp.where(rows == cols, (runs - 1) / inflation, 0.0)
    inverse = inverse_factor(system)
    half_way = dot(right_ref[...], inverse, NT)
    mean_weight = dot(half_way, inverse)
    mixer_ref[...] = mean_weight[0:1] + jnp.sqrt(jnp.float32(runs - 1)) * inverse


def mixer_of(gram, right, sums):
    vmem = pl.BlockSpec(memory_space=pltpu.VMEM)
    return pl.pallas_call(
        mixer_kernel,
        in_specs=[vmem] * 3,
        out_specs=vmem,
        out_shape=jax.ShapeDtypeStruct(gram.shape, jnp.float32),
        compiler_params=pltpu.CompilerParams(vmem_limit_bytes=VMEM_LIMIT),
        name="mixer",
    )(gram, right, sums)


def apply_kernel(mixer_ref, near_ref, far_ref, out_ref):
    sources, half, states, lanes = near_ref.shape
    runs = 2 * sources * half
    high, low = halves(mixer_ref[...])
    wide = jnp.concatenate([high, low, high], axis=1)
    flat = lambda ref: ref.reshape(sources * half * states, lanes)
    near_rows, far_rows = flat(near_ref), flat(far_ref)
    out_rows = out_ref.reshape(runs * states, lanes)

    def members(s):
        parts = [
            rows[pl.ds(s, sources * half, stride=states), :].reshape(sources, half, lanes)
            for rows in (near_rows, far_rows)
        ]
        return jnp.concatenate(parts, axis=1).reshape(runs, lanes)

    for s in range(0, states, 2):
        x = jnp.concatenate([members(s), members(s + 1)], axis=1)
        mean = jnp.sum(x, axis=0, keepdims=True) * (1.0 / runs)
        x_high, x_low = halves(x - mean)
        out = mean + fast_dot(wide, jnp.concatenate([x_high, x_high, x_low], axis=0))
        for i in range(2):
            out_rows[pl.ds(s + i, runs, stride=states), :] = out[:, i * lanes : (i + 1) * lanes]


def apply_mixer(mixer, near, far, chunk=8):
    sources, half, states, lanes = far.shape
    runs = 2 * sources * half
    part = pl.BlockSpec((sources, half, chunk, lanes), lambda g: (0, 0, g, 0))
    return pl.pallas_call(
        apply_kernel,
        grid=(states // chunk,),
        in_specs=[pl.BlockSpec((runs, runs), lambda g: (0, 0)), part, part],
        out_specs=pl.BlockSpec((runs, chunk, lanes), lambda g: (0, g, 0)),
        out_shape=jax.ShapeDtypeStruct((runs, states, lanes), jnp.float32),
        compiler_params=pltpu.CompilerParams(vmem_limit_bytes=VMEM_LIMIT),
        name="apply",
    )(mixer, near, far)


def butterfly_sum(x, axes):
    for axis in axes:
        size = lax.axis_size(axis)
        step = 1
        while step < size:
            x = x + lax.ppermute(x, axis, [(i, i ^ step) for i in range(size)])
            step *= 2
    return x


def on_device(
    ensemble,
    outgoing_fraction,
    mixing,
    downstream_position,
    obs_index,
    obs_value,
    obs_error,
    obs_count,
):
    m, s, r = ensemble.shape
    blocks = r // BL
    reaches = lax.axis_size("reach")
    block = lax.axis_index("mem").astype(jnp.int32).reshape(1)
    routing = (ensemble, outgoing_fraction, downstream_position.reshape(1, r), mixing)
    halo = lax.ppermute(edge_carries(*routing), "reach", [(i, i + 1) for i in range(reaches - 1)])
    near, far = forecast(*routing, obs_index, halo)

    near = lax.all_to_all(near, "mem", split_axis=0, concat_axis=0, tiled=True)
    far = lax.all_to_all(far, "mem", split_axis=0, concat_axis=0, tiled=True)
    gram, right, sums = innovations(block, near, obs_value, obs_error, obs_count, m)
    sums = butterfly_sum(sums, ("reach",))
    mixer = mixer_of(gram, right, sums)
    updated = apply_mixer(mixer, near.reshape(blocks, -1, s, BL), far.reshape(blocks, -1, s, BL))
    returned = lax.all_to_all(
        updated.reshape(blocks, m, s, BL), "mem", split_axis=0, concat_axis=0, tiled=True
    )
    return jnp.transpose(returned, (1, 2, 0, 3)).reshape(m, s, r)


def solution(mesh):
    placed = (
        P("mem", None, "reach"),
        P(None, "reach"),
        P(),
        P("reach"),
        P("reach", None),
        P("reach", None),
        P("reach", None),
        P("reach"),
    )
    return jax.shard_map(
        on_device, mesh=mesh, in_specs=placed, out_specs=P("mem", None, "reach"), check_vma=False
    )
```

```python
import functools

import jax
import jax.numpy as jnp
from jax import lax
from jax.experimental import pallas as pl
from jax.experimental.pallas import tpu as pltpu
from jax.sharding import PartitionSpec as P

BL = 128
HIGHEST = lax.Precision.HIGHEST
NT = (((1,), (1,)), ((), ()))
NN = (((1,), (0,)), ((), ()))
TN = (((0,), (0,)), ((), ()))
VMEM_LIMIT = 16 * 1024 * 1024
SMALL_LIMIT = 8 * 1024 * 1024


def dot(a, b, dims=NN):
    return lax.dot_general(a, b, dims, precision=HIGHEST, preferred_element_type=jnp.float32)


def fast_dot(a, b, dims=NN):
    return lax.dot_general(a, b, dims, preferred_element_type=jnp.float32)


def halves(x):
    high = x.astype(jnp.bfloat16)
    low = (x - high.astype(jnp.float32)).astype(jnp.bfloat16)
    return high, low


def one_hot(index, iota):
    return (index == iota).astype(jnp.float32).astype(jnp.bfloat16)


def target_table(position_row):
    reaches = position_row.shape[1]
    column = jnp.broadcast_to(position_row, (reaches, reaches)).T
    lanes = lax.broadcasted_iota(jnp.int32, (reaches, reaches), 1)
    hot = jnp.concatenate([one_hot(column, lanes), one_hot(column, lanes + reaches)], axis=1)
    return jnp.concatenate([hot, hot], axis=0)


def slot_table(reach_row):
    rows = lax.broadcasted_iota(jnp.int32, (BL, reach_row.shape[1]), 0)
    hot = one_hot(reach_row, rows)
    return jnp.concatenate([hot, hot], axis=0)


def select(x, table):
    m, s, r = x.shape
    high, low = halves(x.reshape(m * s, r))
    out = fast_dot(jnp.concatenate([high, low], axis=1), table)
    return out.reshape(m, s, table.shape[1])


def blend(x, mix3):
    parts = []
    for k in range(0, x.shape[0], 2):
        pair = jnp.concatenate([x[k], x[k + 1]], axis=1)
        high, low = halves(pair)
        out = fast_dot(mix3, jnp.concatenate([high, low, high], axis=0))
        parts += [out[:, :BL], out[:, BL:]]
    return 0.5 * jnp.tanh(jnp.stack(parts))


def prepare_mixing(mixing_ref, mix3_ref):
    s = mixing_ref.shape[0]
    rows = lax.broadcasted_iota(jnp.int32, (s, s), 0)
    cols = lax.broadcasted_iota(jnp.int32, (s, s), 1)
    flipped = dot(mixing_ref[...], (rows == cols).astype(jnp.float32), TN)
    high, low = halves(flipped)
    mix3_ref[...] = jnp.concatenate([high, high, low], axis=1)


def edge_of(x_ref, f_ref, v_ref, mix3):
    outflow = f_ref[:, :BL][None] * x_ref[:, :, :BL]
    arriving = select(outflow, target_table(v_ref[:, :BL]))[:, :, BL:]
    table = target_table(v_ref[:, BL:])
    x = x_ref[:, :, BL:]
    f = f_ref[:, BL:][None]
    outflow = f * x
    routed = select(outflow, table)
    x = x - outflow + (routed[:, :, :BL] + arriving) + blend(x, mix3)
    return routed[:, :, BL:], select(f * x, table)[:, :, BL:]


def edge_kernel(x_ref, f_ref, v_ref, mixing_ref, carry_ref, mix3_ref):
    prepare_mixing(mixing_ref, mix3_ref)
    carry_ref[0], carry_ref[1] = edge_of(x_ref, f_ref, v_ref, mix3_ref[...])


def edge_carries(ensemble, fraction, positions, mixing):
    m, s, r = ensemble.shape
    pair = r // (2 * BL) - 1
    return pl.pallas_call(
        edge_kernel,
        grid=(1,),
        in_specs=[
            pl.BlockSpec((m, s, 2 * BL), lambda g: (0, 0, pair)),
            pl.BlockSpec((s, 2 * BL), lambda g: (0, pair)),
            pl.BlockSpec((1, 2 * BL), lambda g: (0, pair)),
            pl.BlockSpec((s, s), lambda g: (0, 0)),
        ],
        out_specs=pl.BlockSpec((2, m, s, BL), lambda g: (0, 0, 0, 0)),
        out_shape=jax.ShapeDtypeStruct((2, m, s, BL), jnp.float32),
        scratch_shapes=[pltpu.VMEM((s, 3 * s), jnp.bfloat16)],
        compiler_params=pltpu.CompilerParams(vmem_limit_bytes=VMEM_LIMIT),
        name="edge",
    )(ensemble, fraction, positions, mixing)


def forecast_step(x, f, v, slots, mix3, carry_ref):
    m, s, _ = x.shape
    table = target_table(v)
    f = f[None]
    for step in range(2):
        outflow = f * x
        routed = select(outflow, table)
        x = x - outflow + (routed[:, :, :BL] + carry_ref[step]) + blend(x, mix3)
        carry_ref[step] = routed[:, :, BL:]
    state_of = slots // BL
    looked = select(x, slot_table(slots - state_of * BL))
    rows = lax.broadcasted_iota(jnp.int32, (s, slots.shape[1]), 0)
    hot_state = (rows == state_of).astype(jnp.float32)
    seen = jnp.sum(looked * hot_state[None], axis=1)
    mean = jnp.sum(seen, axis=0, keepdims=True) * (1.0 / m)
    pert = seen - mean
    return x, seen, mean, jnp.sum(pert * pert, axis=0, keepdims=True)


def store_block(x, seen, near_ref, far_ref, at):
    m, s, lanes = x.shape
    rows = m // 2 * s
    near_ref[at, :rows, :] = x[: m // 2].reshape(rows, lanes)
    far_ref[at] = x[m // 2 :].reshape(rows, lanes)
    near_ref[at, rows : rows + m, :] = seen[:, :BL]
    near_ref[at, rows + m : rows + 2 * m, :] = seen[:, BL:]


def store_moments(mean, moment, moments_ref, block):
    blocks = moments_ref.shape[0] // 4
    for k, part in enumerate((mean[:, :BL], mean[:, BL:], moment[:, :BL], moment[:, BL:])):
        moments_ref[pl.ds(k * blocks + block, 1), :] = part


def inner_kernel(
    x2_ref, f2_ref, v2_ref, x_ref, f_ref, v_ref, mixing_ref, slot_ref,
    near_ref, far_ref, moments_ref, mix3_ref, carry_ref,
):
    step = pl.program_id(0)

    @pl.when(step == 0)
    def _():
        prepare_mixing(mixing_ref, mix3_ref)
        carry_ref[0], carry_ref[1] = edge_of(x2_ref, f2_ref, v2_ref, mix3_ref[...])

    for i in range(2):
        block = 2 * step + 2 + i
        lanes = slice(i * BL, (i + 1) * BL)
        x, seen, mean, moment = forecast_step(
            x_ref[:, :, lanes], f_ref[:, lanes], v_ref[:, lanes], slot_ref[pl.ds(block, 1), :],
            mix3_ref[...], carry_ref,
        )
        store_block(x, seen, near_ref, far_ref, i)
        store_moments(mean, moment, moments_ref, block)


def outer_kernel(
    x_ref, f_ref, v_ref, mixing_ref, slot_ref, halo_ref, moments_in, near_in, far_in,
    near_ref, far_ref, mix3_ref, carry_ref, near_buffer, far_buffer, moments_buffer, spread_buffer, sems,
):
    blocks = near_ref.shape[0]
    prepare_mixing(mixing_ref, mix3_ref)
    carry_ref[...] = halo_ref[...]
    moments_buffer[...] = moments_in[...]
    for block in range(2):
        lanes = slice(block * BL, (block + 1) * BL)
        x, seen, mean, moment = forecast_step(
            x_ref[:, :, lanes], f_ref[:, lanes], v_ref[:, lanes], slot_ref[block : block + 1, :],
            mix3_ref[...], carry_ref,
        )
        store_block(x, seen, near_buffer, far_buffer, block)
        store_moments(mean, moment, moments_buffer, block)
    first = near_buffer.shape[1] - moments_buffer.shape[0]
    moments = moments_buffer[...]
    near_buffer[:, first:, :] = jnp.broadcast_to(moments[None], (2,) + moments.shape)
    spread_buffer[...] = jnp.broadcast_to(moments[None], spread_buffer.shape)
    copies = [
        pltpu.make_async_copy(near_buffer, near_ref.at[0:2], sems.at[0]),
        pltpu.make_async_copy(far_buffer, far_ref.at[0:2], sems.at[1]),
        pltpu.make_async_copy(
            spread_buffer, near_ref.at[2:blocks, first : first + moments.shape[0], :], sems.at[2]
        ),
    ]
    for copy in copies:
        copy.start()
    for copy in copies:
        copy.wait()


def forecast(ensemble, fraction, positions, mixing, slots, halo):
    m, s, r = ensemble.shape
    blocks, cap = slots.shape
    whole = lambda *shape: pl.BlockSpec(shape, lambda g: (0,) * len(shape))
    held = pl.BlockSpec(memory_space=pl.ANY)
    pair = [whole(m, s, 2 * BL), whole(s, 2 * BL), whole(1, 2 * BL)]
    rows = m // 2 * s
    extra = 2 * m + 4 * blocks
    near = jax.ShapeDtypeStruct((blocks, rows + extra, BL), jnp.float32)
    far = jax.ShapeDtypeStruct((blocks, rows, BL), jnp.float32)
    mix3 = pltpu.VMEM((s, 3 * s), jnp.bfloat16)
    carry = pltpu.VMEM((2, m, s, BL), jnp.float32)
    routing = (ensemble, fraction, positions)
    near_part, far_part, moments = pl.pallas_call(
        inner_kernel,
        grid=(blocks // 2 - 1,),
        in_specs=pair
        + [
            pl.BlockSpec((m, s, 2 * BL), lambda g: (0, 0, g + 1)),
            pl.BlockSpec((s, 2 * BL), lambda g: (0, g + 1)),
            pl.BlockSpec((1, 2 * BL), lambda g: (0, g + 1)),
            whole(s, s),
            whole(blocks, cap),
        ],
        out_specs=[
            pl.BlockSpec((2, rows + extra, BL), lambda g: (g + 1, 0, 0)),
            pl.BlockSpec((2, rows, BL), lambda g: (g + 1, 0, 0)),
            whole(4 * blocks, BL),
        ],
        out_shape=[near, far, jax.ShapeDtypeStruct((4 * blocks, BL), jnp.float32)],
        scratch_shapes=[mix3, carry],
        compiler_params=pltpu.CompilerParams(vmem_limit_bytes=VMEM_LIMIT),
        name="inner",
    )(*routing, *routing, mixing, slots)
    return pl.pallas_call(
        outer_kernel,
        grid=(1,),
        in_specs=pair + [whole(s, s), whole(blocks, cap), whole(2, m, s, BL), whole(4 * blocks, BL), held, held],
        out_specs=[held, held],
        out_shape=[near, far],
        scratch_shapes=[
            mix3,
            carry,
            pltpu.VMEM((2,) + near.shape[1:], jnp.float32),
            pltpu.VMEM((2,) + far.shape[1:], jnp.float32),
            pltpu.VMEM((4 * blocks, BL), jnp.float32),
            pltpu.VMEM((blocks - 2, 4 * blocks, BL), jnp.float32),
            pltpu.SemaphoreType.DMA((3,)),
        ],
        input_output_aliases={7: 0, 8: 1},
        compiler_params=pltpu.CompilerParams(vmem_limit_bytes=VMEM_LIMIT),
        name="outer",
    )(*routing, mixing, slots, halo, moments, near_part, far_part)


def member_order(runs, m, turned):
    rows = lax.broadcasted_iota(jnp.int32, (runs, runs), 0)
    cols = lax.broadcasted_iota(jnp.int32, (runs, runs), 1)
    reversed_rows = runs - m - rows + 2 * (rows % m)
    return (jnp.where(turned == 1, reversed_rows, rows) == cols).astype(jnp.float32)


def innovation_kernel(
    place_ref, count_ref, near_ref, values_ref, errors_ref, gram_ref, right_ref, sums_ref
):
    blocks, cap = values_ref.shape
    sources = near_ref.shape[0]
    m = (near_ref.shape[1] - 4 * blocks) // 2
    runs = sources * m
    joined = lambda at, size: jnp.concatenate(
        [near_ref[:, at : at + size, :], near_ref[:, at + size : at + 2 * size, :]], axis=2
    )
    means = joined(2 * m, blocks)
    mean = jnp.sum(means, axis=0) * (1.0 / sources)
    drift = means - mean[None]
    moment = jnp.sum(joined(2 * m + 2 * blocks, blocks), axis=0) + m * jnp.sum(drift * drift, axis=0)
    spread = moment / (runs - 1)
    lanes = lax.broadcasted_iota(jnp.int32, (blocks, cap), 1)
    rows = lax.broadcasted_iota(jnp.int32, (blocks, cap), 0)
    counts = jnp.zeros((blocks, cap), jnp.int32)
    for k in range(blocks):
        counts = jnp.where(rows == k, count_ref[k], counts)
    live = (lanes < counts).astype(jnp.float32)
    departure = values_ref[...] - mean
    errors = errors_ref[...]
    terms = live * departure * departure / (errors * errors + spread)
    statistic = jnp.sum(jnp.sum(terms, axis=0, keepdims=True), axis=1, keepdims=True)
    total = jnp.sum(counts[:, :1].astype(jnp.float32), axis=0, keepdims=True)
    lanes = lax.broadcasted_iota(jnp.int32, sums_ref.shape, 1)
    sums_ref[...] = jnp.where(lanes < 64, statistic, total)

    own = place_ref[0]
    seen = dot(member_order(runs, m, place_ref[1]), joined(0, m).reshape(runs, cap))
    mean = jnp.sum(seen, axis=0, keepdims=True) * (1.0 / runs)
    pert = seen - mean
    errors = errors_ref[pl.ds(own, 1), :]
    lanes = lax.broadcasted_iota(jnp.int32, (1, cap), 1)
    live = (lanes < count_ref[own]).astype(jnp.float32)
    weighted = pert * (live / (errors * errors))
    departure = values_ref[pl.ds(own, 1), :] - mean
    gram_ref[...] = dot(weighted, pert, NT)
    right_ref[...] = dot(jnp.broadcast_to(departure, (8, cap)), weighted, NT)


def innovations(place, near, values, errors, counts, m):
    blocks, cap = values.shape
    sources, rows, lanes = near.shape
    extra = 2 * m + 4 * blocks
    runs = sources * m
    whole = lambda *shape: pl.BlockSpec(shape, lambda g: (0,) * len(shape))
    smem = pl.BlockSpec(memory_space=pltpu.SMEM)
    return pl.pallas_call(
        innovation_kernel,
        grid=(1,),
        in_specs=[
            smem,
            smem,
            pl.BlockSpec((sources, extra, lanes), lambda g: (0, rows // extra - 1, 0)),
            whole(blocks, cap),
            whole(blocks, cap),
        ],
        out_specs=[whole(runs, runs), whole(8, runs), whole(8, 128)],
        out_shape=[
            jax.ShapeDtypeStruct((runs, runs), jnp.float32),
            jax.ShapeDtypeStruct((8, runs), jnp.float32),
            jax.ShapeDtypeStruct((8, 128), jnp.float32),
        ],
        name="innovation",
    )(place, counts, near, values, errors)


def small_inverse_factor(a):
    n = a.shape[0]
    rows = lax.broadcasted_iota(jnp.int32, (n, n), 0)
    cols = lax.broadcasted_iota(jnp.int32, (n, n), 1)
    both = jnp.concatenate([a, (rows == cols).astype(jnp.float32)], axis=1)
    groups = [both[k : k + 8] for k in range(0, n, 8)]
    sub = lax.broadcasted_iota(jnp.int32, (8, 2 * n), 0)
    lane = lambda x, j: jnp.broadcast_to(x[:, j : j + 1], x.shape)
    line = lambda x, i: jnp.broadcast_to(x[i : i + 1], x.shape)
    scales = []
    for j in range(0, n, 2):
        k, i = divmod(j, 8)
        head = groups[k]
        first = [lane(g, j) for g in groups[k:]]
        second = [lane(g, j + 1) for g in groups[k:]]
        p, q, t = line(first[0], i), line(second[0], i), line(second[0], i + 1)
        top, bottom = line(head, i), line(head, i + 1)
        scale_top = 1.0 / p
        scale_bottom = p * (1.0 / (p * t - q * q))
        slope = q * scale_top
        bottom = bottom - slope * top
        bottom_row = bottom * scale_bottom
        top_row = top * scale_top - slope * bottom_row
        groups[k:] = [
            g - f * top_row - h * bottom_row for g, f, h in zip(groups[k:], first, second)
        ]
        groups[k] = jnp.where(sub > i + 1, groups[k], jnp.where(sub == i + 1, bottom, head))
        if i == 0:
            scales.append(scale_top)
        scales[k] = jnp.where(sub > i, scale_bottom, jnp.where(sub == i, scale_top, scales[k]))
    inverse = jnp.concatenate([g * jnp.sqrt(c) for g, c in zip(groups, scales)], axis=0)
    return inverse[:, n:]


def inverse_factor(a):
    n = a.shape[0]
    if n <= 64:
        return small_inverse_factor(a)
    h = n // 2
    first = inverse_factor(a[:h, :h])
    cross = dot(a[h:, :h], first, NT)
    second = inverse_factor(a[h:, h:] - dot(cross, cross, NT))
    lower = -dot(second, dot(cross, first))
    zero = jnp.zeros((h, h), jnp.float32)
    return jnp.concatenate(
        [jnp.concatenate([first, zero], axis=1), jnp.concatenate([lower, second], axis=1)], axis=0
    )


def mixer_kernel(m, place_ref, gram_ref, right_ref, sums_ref, mixer_ref):
    runs = gram_ref.shape[0]
    inflation = 0.5 + sums_ref[0:1, 0:1] / sums_ref[0:1, 64:65]
    rows = lax.broadcasted_iota(jnp.int32, (runs, runs), 0)
    cols = lax.broadcasted_iota(jnp.int32, (runs, runs), 1)
    system = gram_ref[...] + jnp.where(rows == cols, (runs - 1) / inflation, 0.0)
    inverse = inverse_factor(system)
    half_way = dot(right_ref[...], inverse, NT)
    mean_weight = dot(half_way, inverse)
    mixer = mean_weight[0:1] + jnp.sqrt(jnp.float32(runs - 1)) * inverse
    order = member_order(runs, m, place_ref[1])
    mixer_ref[...] = dot(order, dot(mixer, order, NT))


def mixer_of(place, gram, right, sums, m):
    vmem = pl.BlockSpec(memory_space=pltpu.VMEM)
    return pl.pallas_call(
        functools.partial(mixer_kernel, m),
        in_specs=[pl.BlockSpec(memory_space=pltpu.SMEM)] + [vmem] * 3,
        out_specs=vmem,
        out_shape=jax.ShapeDtypeStruct(gram.shape, jnp.float32),
        compiler_params=pltpu.CompilerParams(vmem_limit_bytes=SMALL_LIMIT),
        name="mixer",
    )(place, gram, right, sums)


def apply_kernel(mixer_ref, near_ref, far_ref, out_ref):
    sources, half, states, lanes = near_ref.shape
    runs = 2 * sources * half
    high, low = halves(mixer_ref[...])
    wide = jnp.concatenate([high, low, high], axis=1)
    flat = lambda ref: ref.reshape(sources * half * states, lanes)
    near_rows, far_rows = flat(near_ref), flat(far_ref)
    out_rows = out_ref.reshape(runs * states, lanes)

    def members(s):
        parts = [
            rows[pl.ds(s, sources * half, stride=states), :].reshape(sources, half, lanes)
            for rows in (near_rows, far_rows)
        ]
        return jnp.concatenate(parts, axis=1).reshape(runs, lanes)

    for s in range(0, states, 2):
        x = jnp.concatenate([members(s), members(s + 1)], axis=1)
        mean = jnp.sum(x, axis=0, keepdims=True) * (1.0 / runs)
        x_high, x_low = halves(x - mean)
        out = mean + fast_dot(wide, jnp.concatenate([x_high, x_high, x_low], axis=0))
        for i in range(2):
            out_rows[pl.ds(s + i, runs, stride=states), :] = out[:, i * lanes : (i + 1) * lanes]


def apply_mixer(mixer, near, far, chunk=8):
    sources, half, states, lanes = far.shape
    runs = 2 * sources * half
    part = pl.BlockSpec((sources, half, chunk, lanes), lambda g: (0, 0, g, 0))
    return pl.pallas_call(
        apply_kernel,
        grid=(states // chunk,),
        in_specs=[pl.BlockSpec((runs, runs), lambda g: (0, 0)), part, part],
        out_specs=pl.BlockSpec((runs, chunk, lanes), lambda g: (0, g, 0)),
        out_shape=jax.ShapeDtypeStruct((runs, states, lanes), jnp.float32),
        compiler_params=pltpu.CompilerParams(vmem_limit_bytes=VMEM_LIMIT),
        name="apply",
    )(mixer, near, far)


def unpack_kernel(x_ref, out_ref, sems):
    copies = [
        pltpu.make_async_copy(x_ref.at[b], out_ref.at[:, :, pl.ds(b * BL, BL)], sems.at[b])
        for b in range(x_ref.shape[0])
    ]
    for copy in copies:
        copy.start()
    for copy in copies:
        copy.wait()


def unpack(x):
    blocks, m, s, lanes = x.shape
    return pl.pallas_call(
        unpack_kernel,
        in_specs=[pl.BlockSpec(memory_space=pltpu.VMEM)],
        out_specs=pl.BlockSpec(memory_space=pl.ANY),
        out_shape=jax.ShapeDtypeStruct((m, s, blocks * lanes), jnp.float32),
        scratch_shapes=[pltpu.SemaphoreType.DMA((blocks,))],
        compiler_params=pltpu.CompilerParams(vmem_limit_bytes=SMALL_LIMIT),
        name="unpack",
    )(x)


def exchange(x):
    size, reaches = lax.axis_size("mem"), lax.axis_size("reach")
    groups = [
        [(size - 1 - i if r % 2 else i) * reaches + r for i in range(size)] for r in range(reaches)
    ]
    return lax.all_to_all(
        x, ("mem", "reach"), split_axis=0, concat_axis=0, tiled=True, axis_index_groups=groups
    )


def butterfly_sum(x, axes):
    for axis in axes:
        size = lax.axis_size(axis)
        step = 1
        while step < size:
            x = x + lax.ppermute(x, axis, [(i, i ^ step) for i in range(size)])
            step *= 2
    return x


def on_device(
    ensemble,
    outgoing_fraction,
    mixing,
    downstream_position,
    obs_index,
    obs_value,
    obs_error,
    obs_count,
):
    m, s, r = ensemble.shape
    blocks = r // BL
    reaches = lax.axis_size("reach")
    mem = lax.axis_index("mem").astype(jnp.int32)
    turned = (lax.axis_index("reach") % 2).astype(jnp.int32)
    block = jnp.where(turned == 1, lax.axis_size("mem") - 1 - mem, mem)
    place = jnp.stack([block, turned])
    routing = (ensemble, outgoing_fraction, downstream_position.reshape(1, r), mixing)
    halo = lax.ppermute(edge_carries(*routing), "reach", [(i, i + 1) for i in range(reaches - 1)])
    near, far = forecast(*routing, obs_index, halo)

    near = exchange(near)
    far = exchange(far)
    gram, right, sums = innovations(place, near, obs_value, obs_error, obs_count, m)
    sums = butterfly_sum(sums, ("reach",))
    mixer = mixer_of(place, gram, right, sums, m)
    updated = apply_mixer(mixer, near.reshape(blocks, -1, s, BL), far.reshape(blocks, -1, s, BL))
    returned = exchange(updated.reshape(blocks, m, s, BL))
    return unpack(returned)


def solution(mesh):
    placed = (
        P("mem", None, "reach"),
        P(None, "reach"),
        P(),
        P("reach"),
        P("reach", None),
        P("reach", None),
        P("reach", None),
        P("reach"),
    )
    return jax.shard_map(
        on_device, mesh=mesh, in_specs=placed, out_specs=P("mem", None, "reach"), check_vma=False
    )
```

```python
import functools

import jax
import jax.numpy as jnp
from jax import lax
from jax.experimental import pallas as pl
from jax.experimental.pallas import tpu as pltpu
from jax.sharding import PartitionSpec as P

BL = 128
HIGHEST = lax.Precision.HIGHEST
NT = (((1,), (1,)), ((), ()))
NN = (((1,), (0,)), ((), ()))
TN = (((0,), (0,)), ((), ()))
VMEM_LIMIT = 16 * 1024 * 1024
SMALL_LIMIT = 8 * 1024 * 1024


def dot(a, b, dims=NN):
    return lax.dot_general(a, b, dims, precision=HIGHEST, preferred_element_type=jnp.float32)


def fast_dot(a, b, dims=NN):
    return lax.dot_general(a, b, dims, preferred_element_type=jnp.float32)


def halves(x):
    high = x.astype(jnp.bfloat16)
    low = (x - high.astype(jnp.float32)).astype(jnp.bfloat16)
    return high, low


def one_hot(index, iota):
    return (index == iota).astype(jnp.float32).astype(jnp.bfloat16)


def target_table(position_row):
    reaches = position_row.shape[1]
    column = jnp.broadcast_to(position_row, (reaches, reaches)).T
    lanes = lax.broadcasted_iota(jnp.int32, (reaches, reaches), 1)
    hot = jnp.concatenate([one_hot(column, lanes), one_hot(column, lanes + reaches)], axis=1)
    return jnp.concatenate([hot, hot], axis=0)


def slot_table(reach_row):
    rows = lax.broadcasted_iota(jnp.int32, (BL, reach_row.shape[1]), 0)
    hot = one_hot(reach_row, rows)
    return jnp.concatenate([hot, hot], axis=0)


def select(x, table):
    m, s, r = x.shape
    high, low = halves(x.reshape(m * s, r))
    out = fast_dot(jnp.concatenate([high, low], axis=1), table)
    return out.reshape(m, s, table.shape[1])


def blend(x, mix3):
    parts = []
    for k in range(0, x.shape[0], 2):
        pair = jnp.concatenate([x[k], x[k + 1]], axis=1)
        high, low = halves(pair)
        out = fast_dot(mix3, jnp.concatenate([high, low, high], axis=0))
        parts += [out[:, :BL], out[:, BL:]]
    return 0.5 * jnp.tanh(jnp.stack(parts))


def prepare_mixing(mixing_ref, mix3_ref):
    s = mixing_ref.shape[0]
    rows = lax.broadcasted_iota(jnp.int32, (s, s), 0)
    cols = lax.broadcasted_iota(jnp.int32, (s, s), 1)
    flipped = dot(mixing_ref[...], (rows == cols).astype(jnp.float32), TN)
    high, low = halves(flipped)
    mix3_ref[...] = jnp.concatenate([high, high, low], axis=1)


def edge_of(x_ref, f_ref, v_ref, mix3):
    outflow = f_ref[:, :BL][None] * x_ref[:, :, :BL]
    arriving = select(outflow, target_table(v_ref[:, :BL]))[:, :, BL:]
    table = target_table(v_ref[:, BL:])
    x = x_ref[:, :, BL:]
    f = f_ref[:, BL:][None]
    outflow = f * x
    routed = select(outflow, table)
    x = x - outflow + (routed[:, :, :BL] + arriving) + blend(x, mix3)
    return routed[:, :, BL:], select(f * x, table)[:, :, BL:]


def edge_kernel(x_ref, f_ref, v_ref, mixing_ref, carry_ref, mix3_ref):
    prepare_mixing(mixing_ref, mix3_ref)
    carry_ref[0], carry_ref[1] = edge_of(x_ref, f_ref, v_ref, mix3_ref[...])


def edge_carries(ensemble, fraction, positions, mixing):
    m, s, r = ensemble.shape
    pair = r // (2 * BL) - 1
    return pl.pallas_call(
        edge_kernel,
        grid=(1,),
        in_specs=[
            pl.BlockSpec((m, s, 2 * BL), lambda g: (0, 0, pair)),
            pl.BlockSpec((s, 2 * BL), lambda g: (0, pair)),
            pl.BlockSpec((1, 2 * BL), lambda g: (0, pair)),
            pl.BlockSpec((s, s), lambda g: (0, 0)),
        ],
        out_specs=pl.BlockSpec((2, m, s, BL), lambda g: (0, 0, 0, 0)),
        out_shape=jax.ShapeDtypeStruct((2, m, s, BL), jnp.float32),
        scratch_shapes=[pltpu.VMEM((s, 3 * s), jnp.bfloat16)],
        compiler_params=pltpu.CompilerParams(vmem_limit_bytes=VMEM_LIMIT),
        name="edge",
    )(ensemble, fraction, positions, mixing)


def forecast_step(x, f, v, slots, mix3, carry_ref):
    m, s, _ = x.shape
    table = target_table(v)
    f = f[None]
    for step in range(2):
        outflow = f * x
        routed = select(outflow, table)
        x = x - outflow + (routed[:, :, :BL] + carry_ref[step]) + blend(x, mix3)
        carry_ref[step] = routed[:, :, BL:]
    state_of = slots // BL
    looked = select(x, slot_table(slots - state_of * BL))
    rows = lax.broadcasted_iota(jnp.int32, (s, slots.shape[1]), 0)
    hot_state = (rows == state_of).astype(jnp.float32)
    seen = jnp.sum(looked * hot_state[None], axis=1)
    mean = jnp.sum(seen, axis=0, keepdims=True) * (1.0 / m)
    pert = seen - mean
    return x, seen, mean, jnp.sum(pert * pert, axis=0, keepdims=True)


def store_block(x, seen, near_ref, far_ref, at):
    m, s, lanes = x.shape
    rows = m // 2 * s
    near_ref[at, :rows, :] = x[: m // 2].reshape(rows, lanes)
    far_ref[at] = x[m // 2 :].reshape(rows, lanes)
    near_ref[at, rows : rows + m, :] = seen[:, :BL]
    near_ref[at, rows + m : rows + 2 * m, :] = seen[:, BL:]


def store_moments(mean, moment, moments_ref, block):
    blocks = moments_ref.shape[0] // 4
    for k, part in enumerate((mean[:, :BL], mean[:, BL:], moment[:, :BL], moment[:, BL:])):
        moments_ref[pl.ds(k * blocks + block, 1), :] = part


def inner_kernel(
    x2_ref, f2_ref, v2_ref, x_ref, f_ref, v_ref, mixing_ref, slot_ref,
    near_ref, far_ref, moments_ref, mix3_ref, carry_ref,
):
    step = pl.program_id(0)

    @pl.when(step == 0)
    def _():
        prepare_mixing(mixing_ref, mix3_ref)
        carry_ref[0], carry_ref[1] = edge_of(x2_ref, f2_ref, v2_ref, mix3_ref[...])

    for i in range(2):
        block = 2 * step + 2 + i
        lanes = slice(i * BL, (i + 1) * BL)
        x, seen, mean, moment = forecast_step(
            x_ref[:, :, lanes], f_ref[:, lanes], v_ref[:, lanes], slot_ref[pl.ds(block, 1), :],
            mix3_ref[...], carry_ref,
        )
        store_block(x, seen, near_ref, far_ref, i)
        store_moments(mean, moment, moments_ref, block)


def outer_kernel(
    x_ref, f_ref, v_ref, mixing_ref, slot_ref, halo_ref, moments_in, near_in, far_in,
    near_ref, far_ref, mix3_ref, carry_ref, near_buffer, far_buffer, moments_buffer, spread_buffer, sems,
):
    blocks = near_ref.shape[0]
    prepare_mixing(mixing_ref, mix3_ref)
    carry_ref[...] = halo_ref[...]
    moments_buffer[...] = moments_in[...]
    for block in range(2):
        lanes = slice(block * BL, (block + 1) * BL)
        x, seen, mean, moment = forecast_step(
            x_ref[:, :, lanes], f_ref[:, lanes], v_ref[:, lanes], slot_ref[block : block + 1, :],
            mix3_ref[...], carry_ref,
        )
        store_block(x, seen, near_buffer, far_buffer, block)
        store_moments(mean, moment, moments_buffer, block)
    first = near_buffer.shape[1] - moments_buffer.shape[0]
    moments = moments_buffer[...]
    near_buffer[:, first:, :] = jnp.broadcast_to(moments[None], (2,) + moments.shape)
    spread_buffer[...] = jnp.broadcast_to(moments[None], spread_buffer.shape)
    copies = [
        pltpu.make_async_copy(near_buffer, near_ref.at[0:2], sems.at[0]),
        pltpu.make_async_copy(far_buffer, far_ref.at[0:2], sems.at[1]),
        pltpu.make_async_copy(
            spread_buffer, near_ref.at[2:blocks, first : first + moments.shape[0], :], sems.at[2]
        ),
    ]
    for copy in copies:
        copy.start()
    for copy in copies:
        copy.wait()


def forecast(ensemble, fraction, positions, mixing, slots, halo):
    m, s, r = ensemble.shape
    blocks, cap = slots.shape
    whole = lambda *shape: pl.BlockSpec(shape, lambda g: (0,) * len(shape))
    held = pl.BlockSpec(memory_space=pl.ANY)
    pair = [whole(m, s, 2 * BL), whole(s, 2 * BL), whole(1, 2 * BL)]
    rows = m // 2 * s
    extra = 2 * m + 4 * blocks
    near = jax.ShapeDtypeStruct((blocks, rows + extra, BL), jnp.float32)
    far = jax.ShapeDtypeStruct((blocks, rows, BL), jnp.float32)
    mix3 = pltpu.VMEM((s, 3 * s), jnp.bfloat16)
    carry = pltpu.VMEM((2, m, s, BL), jnp.float32)
    routing = (ensemble, fraction, positions)
    near_part, far_part, moments = pl.pallas_call(
        inner_kernel,
        grid=(blocks // 2 - 1,),
        in_specs=pair
        + [
            pl.BlockSpec((m, s, 2 * BL), lambda g: (0, 0, g + 1)),
            pl.BlockSpec((s, 2 * BL), lambda g: (0, g + 1)),
            pl.BlockSpec((1, 2 * BL), lambda g: (0, g + 1)),
            whole(s, s),
            whole(blocks, cap),
        ],
        out_specs=[
            pl.BlockSpec((2, rows + extra, BL), lambda g: (g + 1, 0, 0)),
            pl.BlockSpec((2, rows, BL), lambda g: (g + 1, 0, 0)),
            whole(4 * blocks, BL),
        ],
        out_shape=[near, far, jax.ShapeDtypeStruct((4 * blocks, BL), jnp.float32)],
        scratch_shapes=[mix3, carry],
        compiler_params=pltpu.CompilerParams(vmem_limit_bytes=VMEM_LIMIT),
        name="inner",
    )(*routing, *routing, mixing, slots)
    return pl.pallas_call(
        outer_kernel,
        grid=(1,),
        in_specs=pair + [whole(s, s), whole(blocks, cap), whole(2, m, s, BL), whole(4 * blocks, BL), held, held],
        out_specs=[held, held],
        out_shape=[near, far],
        scratch_shapes=[
            mix3,
            carry,
            pltpu.VMEM((2,) + near.shape[1:], jnp.float32),
            pltpu.VMEM((2,) + far.shape[1:], jnp.float32),
            pltpu.VMEM((4 * blocks, BL), jnp.float32),
            pltpu.VMEM((blocks - 2, 4 * blocks, BL), jnp.float32),
            pltpu.SemaphoreType.DMA((3,)),
        ],
        input_output_aliases={7: 0, 8: 1},
        compiler_params=pltpu.CompilerParams(vmem_limit_bytes=VMEM_LIMIT),
        name="outer",
    )(*routing, mixing, slots, halo, moments, near_part, far_part)


def member_order(runs, m, turned):
    rows = lax.broadcasted_iota(jnp.int32, (runs, runs), 0)
    cols = lax.broadcasted_iota(jnp.int32, (runs, runs), 1)
    reversed_rows = runs - m - rows + 2 * (rows % m)
    return (jnp.where(turned == 1, reversed_rows, rows) == cols).astype(jnp.float32)


def innovation_kernel(
    place_ref, count_ref, near_ref, values_ref, errors_ref, gram_ref, sums_ref
):
    blocks, cap = values_ref.shape
    sources = near_ref.shape[0]
    m = (near_ref.shape[1] - 4 * blocks) // 2
    runs = sources * m
    joined = lambda at, size: jnp.concatenate(
        [near_ref[:, at : at + size, :], near_ref[:, at + size : at + 2 * size, :]], axis=2
    )
    means = joined(2 * m, blocks)
    mean = jnp.sum(means, axis=0) * (1.0 / sources)
    drift = means - mean[None]
    moment = jnp.sum(joined(2 * m + 2 * blocks, blocks), axis=0) + m * jnp.sum(drift * drift, axis=0)
    spread = moment / (runs - 1)
    lanes = lax.broadcasted_iota(jnp.int32, (blocks, cap), 1)
    rows = lax.broadcasted_iota(jnp.int32, (blocks, cap), 0)
    counts = jnp.zeros((blocks, cap), jnp.int32)
    for k in range(blocks):
        counts = jnp.where(rows == k, count_ref[k], counts)
    live = (lanes < counts).astype(jnp.float32)
    departure = values_ref[...] - mean
    errors = errors_ref[...]
    terms = live * departure * departure / (errors * errors + spread)
    statistic = jnp.sum(jnp.sum(terms, axis=0, keepdims=True), axis=1, keepdims=True)
    total = jnp.sum(counts[:, :1].astype(jnp.float32), axis=0, keepdims=True)
    lanes = lax.broadcasted_iota(jnp.int32, sums_ref.shape, 1)
    sums_ref[...] = jnp.where(lanes < 64, statistic, total)

    own = lax.shift_right_logical(place_ref[0], 1)
    seen = dot(member_order(runs, m, place_ref[0] & 1), joined(0, m).reshape(runs, cap))
    mean = jnp.sum(seen, axis=0, keepdims=True) * (1.0 / runs)
    pert = seen - mean
    errors = errors_ref[pl.ds(own, 1), :]
    lanes = lax.broadcasted_iota(jnp.int32, (1, cap), 1)
    live = (lanes < count_ref[own]).astype(jnp.float32)
    weighted = pert * (live / (errors * errors))
    departure = values_ref[pl.ds(own, 1), :] - mean
    gram_ref[:runs, :] = dot(weighted, pert, NT)
    gram_ref[runs:, :] = dot(jnp.broadcast_to(departure, (8, cap)), weighted, NT)


def innovations(place, near, values, errors, counts, m):
    blocks, cap = values.shape
    sources, rows, lanes = near.shape
    extra = 2 * m + 4 * blocks
    runs = sources * m
    whole = lambda *shape: pl.BlockSpec(shape, lambda g: (0,) * len(shape))
    smem = pl.BlockSpec(memory_space=pltpu.SMEM)
    return pl.pallas_call(
        innovation_kernel,
        grid=(1,),
        in_specs=[
            smem,
            smem,
            pl.BlockSpec((sources, extra, lanes), lambda g: (0, rows // extra - 1, 0)),
            whole(blocks, cap),
            whole(blocks, cap),
        ],
        out_specs=[whole(runs + 8, runs), whole(8, 128)],
        out_shape=[
            jax.ShapeDtypeStruct((runs + 8, runs), jnp.float32),
            jax.ShapeDtypeStruct((8, 128), jnp.float32),
        ],
        name="innovation",
    )(place, counts, near, values, errors)


def small_inverse_factor(a):
    n = a.shape[0]
    rows = lax.broadcasted_iota(jnp.int32, (n, n), 0)
    cols = lax.broadcasted_iota(jnp.int32, (n, n), 1)
    both = jnp.concatenate([a, (rows == cols).astype(jnp.float32)], axis=1)
    groups = [both[k : k + 8] for k in range(0, n, 8)]
    sub = lax.broadcasted_iota(jnp.int32, (8, 2 * n), 0)
    lane = lambda x, j: jnp.broadcast_to(x[:, j : j + 1], x.shape)
    line = lambda x, i: jnp.broadcast_to(x[i : i + 1], x.shape)
    scales = []
    for j in range(0, n, 2):
        k, i = divmod(j, 8)
        head = groups[k]
        first = [lane(g, j) for g in groups[k:]]
        second = [lane(g, j + 1) for g in groups[k:]]
        p, q, t = line(first[0], i), line(second[0], i), line(second[0], i + 1)
        top, bottom = line(head, i), line(head, i + 1)
        scale_top = 1.0 / p
        scale_bottom = p * (1.0 / (p * t - q * q))
        slope = q * scale_top
        bottom = bottom - slope * top
        bottom_row = bottom * scale_bottom
        top_row = top * scale_top - slope * bottom_row
        groups[k:] = [
            g - f * top_row - h * bottom_row for g, f, h in zip(groups[k:], first, second)
        ]
        groups[k] = jnp.where(sub > i + 1, groups[k], jnp.where(sub == i + 1, bottom, head))
        if i == 0:
            scales.append(scale_top)
        scales[k] = jnp.where(sub > i, scale_bottom, jnp.where(sub == i, scale_top, scales[k]))
    inverse = jnp.concatenate([g * jnp.sqrt(c) for g, c in zip(groups, scales)], axis=0)
    return inverse[:, n:]


def inverse_factor(a):
    n = a.shape[0]
    if n <= 64:
        return small_inverse_factor(a)
    h = n // 2
    first = inverse_factor(a[:h, :h])
    cross = dot(a[h:, :h], first, NT)
    second = inverse_factor(a[h:, h:] - dot(cross, cross, NT))
    lower = -dot(second, dot(cross, first))
    zero = jnp.zeros((h, h), jnp.float32)
    return jnp.concatenate(
        [jnp.concatenate([first, zero], axis=1), jnp.concatenate([lower, second], axis=1)], axis=0
    )


def mixer_kernel(m, place_ref, gram_ref, sums_ref, mixer_ref):
    runs = gram_ref.shape[1]
    inflation = 0.5 + sums_ref[0:1, 0:1] / sums_ref[0:1, 64:65]
    rows = lax.broadcasted_iota(jnp.int32, (runs, runs), 0)
    cols = lax.broadcasted_iota(jnp.int32, (runs, runs), 1)
    system = gram_ref[:runs, :] + jnp.where(rows == cols, (runs - 1) / inflation, 0.0)
    inverse = inverse_factor(system)
    half_way = dot(gram_ref[runs:, :], inverse, NT)
    mean_weight = dot(half_way, inverse)
    mixer = mean_weight[0:1] + jnp.sqrt(jnp.float32(runs - 1)) * inverse
    turned = place_ref[0] & 1
    mixer = dot(mixer, member_order(runs, m, turned), NT)
    groups = runs // m
    for g in range(groups):
        spot = jnp.where(turned == 1, groups - 1 - g, g)
        mixer_ref[pl.ds(pl.multiple_of(spot * m, m), m), :] = mixer[g * m : (g + 1) * m]


def mixer_of(place, gram, sums, m):
    vmem = pl.BlockSpec(memory_space=pltpu.VMEM)
    return pl.pallas_call(
        functools.partial(mixer_kernel, m),
        in_specs=[pl.BlockSpec(memory_space=pltpu.SMEM)] + [vmem] * 2,
        out_specs=vmem,
        out_shape=jax.ShapeDtypeStruct((gram.shape[1],) * 2, jnp.float32),
        compiler_params=pltpu.CompilerParams(vmem_limit_bytes=SMALL_LIMIT),
        name="mixer",
    )(place, gram, sums)


def apply_kernel(mixer_ref, near_ref, far_ref, out_ref):
    sources, half, states, lanes = near_ref.shape
    runs = 2 * sources * half
    high, low = halves(mixer_ref[...])
    wide = jnp.concatenate([high, low, high], axis=1)
    flat = lambda ref: ref.reshape(sources * half * states, lanes)
    near_rows, far_rows = flat(near_ref), flat(far_ref)
    out_rows = out_ref.reshape(runs * states, lanes)

    def members(s):
        parts = [
            rows[pl.ds(s, sources * half, stride=states), :].reshape(sources, half, lanes)
            for rows in (near_rows, far_rows)
        ]
        return jnp.concatenate(parts, axis=1).reshape(runs, lanes)

    for s in range(0, states, 2):
        x = jnp.concatenate([members(s), members(s + 1)], axis=1)
        mean = jnp.sum(x, axis=0, keepdims=True) * (1.0 / runs)
        x_high, x_low = halves(x - mean)
        out = mean + fast_dot(wide, jnp.concatenate([x_high, x_high, x_low], axis=0))
        for i in range(2):
            out_rows[pl.ds(s + i, runs, stride=states), :] = out[:, i * lanes : (i + 1) * lanes]


def apply_mixer(mixer, near, far, chunk=8):
    sources, half, states, lanes = far.shape
    runs = 2 * sources * half
    part = pl.BlockSpec((sources, half, chunk, lanes), lambda g: (0, 0, g, 0))
    return pl.pallas_call(
        apply_kernel,
        grid=(states // chunk,),
        in_specs=[pl.BlockSpec((runs, runs), lambda g: (0, 0)), part, part],
        out_specs=pl.BlockSpec((runs, chunk, lanes), lambda g: (0, g, 0)),
        out_shape=jax.ShapeDtypeStruct((runs, states, lanes), jnp.float32),
        compiler_params=pltpu.CompilerParams(vmem_limit_bytes=VMEM_LIMIT),
        name="apply",
    )(mixer, near, far)


def unpack_kernel(x_ref, out_ref, sems):
    copies = [
        pltpu.make_async_copy(x_ref.at[b], out_ref.at[:, :, pl.ds(b * BL, BL)], sems.at[b])
        for b in range(x_ref.shape[0])
    ]
    for copy in copies:
        copy.start()
    for copy in copies:
        copy.wait()


def unpack(x):
    blocks, m, s, lanes = x.shape
    return pl.pallas_call(
        unpack_kernel,
        in_specs=[pl.BlockSpec(memory_space=pltpu.VMEM)],
        out_specs=pl.BlockSpec(memory_space=pl.ANY),
        out_shape=jax.ShapeDtypeStruct((m, s, blocks * lanes), jnp.float32),
        scratch_shapes=[pltpu.SemaphoreType.DMA((blocks,))],
        compiler_params=pltpu.CompilerParams(vmem_limit_bytes=SMALL_LIMIT),
        name="unpack",
    )(x)


def exchange(x):
    size, reaches = lax.axis_size("mem"), lax.axis_size("reach")
    groups = [
        [(size - 1 - i if r % 2 else i) * reaches + r for i in range(size)] for r in range(reaches)
    ]
    return lax.all_to_all(
        x, ("mem", "reach"), split_axis=0, concat_axis=0, tiled=True, axis_index_groups=groups
    )


def butterfly_sum(x, axes):
    for axis in axes:
        size = lax.axis_size(axis)
        step = 1
        while step < size:
            x = x + lax.ppermute(x, axis, [(i, i ^ step) for i in range(size)])
            step *= 2
    return x


def on_device(
    ensemble,
    outgoing_fraction,
    mixing,
    downstream_position,
    obs_index,
    obs_value,
    obs_error,
    obs_count,
):
    m, s, r = ensemble.shape
    blocks = r // BL
    reaches = lax.axis_size("reach")
    mem = lax.axis_index("mem").astype(jnp.int32)
    turned = (lax.axis_index("reach") % 2).astype(jnp.int32)
    block = jnp.where(turned == 1, lax.axis_size("mem") - 1 - mem, mem)
    place = (2 * block + turned).reshape(1)
    routing = (ensemble, outgoing_fraction, downstream_position.reshape(1, r), mixing)
    halo = lax.ppermute(edge_carries(*routing), "reach", [(i, i + 1) for i in range(reaches - 1)])
    near, far = forecast(*routing, obs_index, halo)

    near = exchange(near)
    far = exchange(far)
    gram, sums = innovations(place, near, obs_value, obs_error, obs_count, m)
    sums = butterfly_sum(sums, ("reach",))
    mixer = mixer_of(place, gram, sums, m)
    updated = apply_mixer(mixer, near.reshape(blocks, -1, s, BL), far.reshape(blocks, -1, s, BL))
    returned = exchange(updated.reshape(blocks, m, s, BL))
    return unpack(returned)


def solution(mesh):
    placed = (
        P("mem", None, "reach"),
        P(None, "reach"),
        P(),
        P("reach"),
        P("reach", None),
        P("reach", None),
        P("reach", None),
        P("reach"),
    )
    return jax.shard_map(
        on_device, mesh=mesh, in_specs=placed, out_specs=P("mem", None, "reach"), check_vma=False
    )
```

```python
import functools

import jax
import jax.numpy as jnp
from jax import lax
from jax.experimental import pallas as pl
from jax.experimental.pallas import tpu as pltpu
from jax.sharding import PartitionSpec as P

BL = 128
HIGHEST = lax.Precision.HIGHEST
NT = (((1,), (1,)), ((), ()))
NN = (((1,), (0,)), ((), ()))
TN = (((0,), (0,)), ((), ()))
VMEM_LIMIT = 16 * 1024 * 1024
SMALL_LIMIT = 8 * 1024 * 1024


def dot(a, b, dims=NN):
    return lax.dot_general(a, b, dims, precision=HIGHEST, preferred_element_type=jnp.float32)


def fast_dot(a, b, dims=NN):
    return lax.dot_general(a, b, dims, preferred_element_type=jnp.float32)


def halves(x):
    high = x.astype(jnp.bfloat16)
    low = (x - high.astype(jnp.float32)).astype(jnp.bfloat16)
    return high, low


def one_hot(index, iota):
    return (index == iota).astype(jnp.float32).astype(jnp.bfloat16)


def target_table(position_row):
    reaches = position_row.shape[1]
    column = jnp.broadcast_to(position_row, (reaches, reaches)).T
    lanes = lax.broadcasted_iota(jnp.int32, (reaches, reaches), 1)
    hot = jnp.concatenate([one_hot(column, lanes), one_hot(column, lanes + reaches)], axis=1)
    return jnp.concatenate([hot, hot], axis=0)


def slot_table(reach_row):
    rows = lax.broadcasted_iota(jnp.int32, (BL, reach_row.shape[1]), 0)
    hot = one_hot(reach_row, rows)
    return jnp.concatenate([hot, hot], axis=0)


def select(x, table):
    m, s, r = x.shape
    high, low = halves(x.reshape(m * s, r))
    out = fast_dot(jnp.concatenate([high, low], axis=1), table)
    return out.reshape(m, s, table.shape[1])


def blend(x, mix3):
    parts = []
    for k in range(0, x.shape[0], 2):
        pair = jnp.concatenate([x[k], x[k + 1]], axis=1)
        high, low = halves(pair)
        out = fast_dot(mix3, jnp.concatenate([high, low, high], axis=0))
        parts += [out[:, :BL], out[:, BL:]]
    return 0.5 * jnp.tanh(jnp.stack(parts))


def prepare_mixing(mixing_ref, mix3_ref):
    s = mixing_ref.shape[0]
    rows = lax.broadcasted_iota(jnp.int32, (s, s), 0)
    cols = lax.broadcasted_iota(jnp.int32, (s, s), 1)
    flipped = dot(mixing_ref[...], (rows == cols).astype(jnp.float32), TN)
    high, low = halves(flipped)
    mix3_ref[...] = jnp.concatenate([high, high, low], axis=1)


def edge_of(x_ref, f_ref, v_ref, mix3):
    outflow = f_ref[:, :BL][None] * x_ref[:, :, :BL]
    arriving = select(outflow, target_table(v_ref[:, :BL]))[:, :, BL:]
    table = target_table(v_ref[:, BL:])
    x = x_ref[:, :, BL:]
    f = f_ref[:, BL:][None]
    outflow = f * x
    routed = select(outflow, table)
    x = x - outflow + (routed[:, :, :BL] + arriving) + blend(x, mix3)
    return routed[:, :, BL:], select(f * x, table)[:, :, BL:]


def edge_kernel(x_ref, f_ref, v_ref, mixing_ref, carry_ref, mix3_ref):
    prepare_mixing(mixing_ref, mix3_ref)
    carry_ref[0], carry_ref[1] = edge_of(x_ref, f_ref, v_ref, mix3_ref[...])


def edge_carries(ensemble, fraction, positions, mixing):
    m, s, r = ensemble.shape
    pair = r // (2 * BL) - 1
    return pl.pallas_call(
        edge_kernel,
        grid=(1,),
        in_specs=[
            pl.BlockSpec((m, s, 2 * BL), lambda g: (0, 0, pair)),
            pl.BlockSpec((s, 2 * BL), lambda g: (0, pair)),
            pl.BlockSpec((1, 2 * BL), lambda g: (0, pair)),
            pl.BlockSpec((s, s), lambda g: (0, 0)),
        ],
        out_specs=pl.BlockSpec((2, m, s, BL), lambda g: (0, 0, 0, 0)),
        out_shape=jax.ShapeDtypeStruct((2, m, s, BL), jnp.float32),
        scratch_shapes=[pltpu.VMEM((s, 3 * s), jnp.bfloat16)],
        compiler_params=pltpu.CompilerParams(vmem_limit_bytes=VMEM_LIMIT),
        name="edge",
    )(ensemble, fraction, positions, mixing)


def forecast_step(x, f, v, slots, mix3, carry_ref):
    m, s, _ = x.shape
    table = target_table(v)
    f = f[None]
    for step in range(2):
        outflow = f * x
        routed = select(outflow, table)
        x = x - outflow + (routed[:, :, :BL] + carry_ref[step]) + blend(x, mix3)
        carry_ref[step] = routed[:, :, BL:]
    state_of = slots // BL
    looked = select(x, slot_table(slots - state_of * BL))
    rows = lax.broadcasted_iota(jnp.int32, (s, slots.shape[1]), 0)
    hot_state = (rows == state_of).astype(jnp.float32)
    seen = jnp.sum(looked * hot_state[None], axis=1)
    mean = jnp.sum(seen, axis=0, keepdims=True) * (1.0 / m)
    pert = seen - mean
    return x, seen, mean, jnp.sum(pert * pert, axis=0, keepdims=True)


def store_block(x, seen, near_ref, far_ref, at):
    m, s, lanes = x.shape
    rows = m // 2 * s
    near_ref[at, :rows, :] = x[: m // 2].reshape(rows, lanes)
    far_ref[at] = x[m // 2 :].reshape(rows, lanes)
    near_ref[at, rows : rows + m, :] = seen[:, :BL]
    near_ref[at, rows + m : rows + 2 * m, :] = seen[:, BL:]


def store_moments(mean, moment, moments_ref, block):
    blocks = moments_ref.shape[0] // 4
    for k, part in enumerate((mean[:, :BL], mean[:, BL:], moment[:, :BL], moment[:, BL:])):
        moments_ref[pl.ds(k * blocks + block, 1), :] = part


def inner_kernel(
    x2_ref, f2_ref, v2_ref, x_ref, f_ref, v_ref, mixing_ref, slot_ref,
    near_ref, far_ref, moments_ref, mix3_ref, carry_ref,
):
    step = pl.program_id(0)

    @pl.when(step == 0)
    def _():
        prepare_mixing(mixing_ref, mix3_ref)
        carry_ref[0], carry_ref[1] = edge_of(x2_ref, f2_ref, v2_ref, mix3_ref[...])

    for i in range(2):
        block = 2 * step + 2 + i
        lanes = slice(i * BL, (i + 1) * BL)
        x, seen, mean, moment = forecast_step(
            x_ref[:, :, lanes], f_ref[:, lanes], v_ref[:, lanes], slot_ref[pl.ds(block, 1), :],
            mix3_ref[...], carry_ref,
        )
        store_block(x, seen, near_ref, far_ref, i)
        store_moments(mean, moment, moments_ref, block)


def outer_kernel(
    x_ref, f_ref, v_ref, mixing_ref, slot_ref, halo_ref, moments_in, near_in, far_in,
    near_ref, far_ref, mix3_ref, carry_ref, near_buffer, far_buffer, moments_buffer, spread_buffer, sems,
):
    blocks = near_ref.shape[0]
    prepare_mixing(mixing_ref, mix3_ref)
    carry_ref[...] = halo_ref[...]
    moments_buffer[...] = moments_in[...]
    for block in range(2):
        lanes = slice(block * BL, (block + 1) * BL)
        x, seen, mean, moment = forecast_step(
            x_ref[:, :, lanes], f_ref[:, lanes], v_ref[:, lanes], slot_ref[block : block + 1, :],
            mix3_ref[...], carry_ref,
        )
        store_block(x, seen, near_buffer, far_buffer, block)
        store_moments(mean, moment, moments_buffer, block)
    first = near_buffer.shape[1] - moments_buffer.shape[0]
    moments = moments_buffer[...]
    near_buffer[:, first:, :] = jnp.broadcast_to(moments[None], (2,) + moments.shape)
    spread_buffer[...] = jnp.broadcast_to(moments[None], spread_buffer.shape)
    copies = [
        pltpu.make_async_copy(near_buffer, near_ref.at[0:2], sems.at[0]),
        pltpu.make_async_copy(far_buffer, far_ref.at[0:2], sems.at[1]),
        pltpu.make_async_copy(
            spread_buffer, near_ref.at[2:blocks, first : first + moments.shape[0], :], sems.at[2]
        ),
    ]
    for copy in copies:
        copy.start()
    for copy in copies:
        copy.wait()


def forecast(ensemble, fraction, positions, mixing, slots, halo):
    m, s, r = ensemble.shape
    blocks, cap = slots.shape
    whole = lambda *shape: pl.BlockSpec(shape, lambda g: (0,) * len(shape))
    held = pl.BlockSpec(memory_space=pl.ANY)
    pair = [whole(m, s, 2 * BL), whole(s, 2 * BL), whole(1, 2 * BL)]
    rows = m // 2 * s
    extra = 2 * m + 4 * blocks
    near = jax.ShapeDtypeStruct((blocks, rows + extra, BL), jnp.float32)
    far = jax.ShapeDtypeStruct((blocks, rows, BL), jnp.float32)
    mix3 = pltpu.VMEM((s, 3 * s), jnp.bfloat16)
    carry = pltpu.VMEM((2, m, s, BL), jnp.float32)
    routing = (ensemble, fraction, positions)
    near_part, far_part, moments = pl.pallas_call(
        inner_kernel,
        grid=(blocks // 2 - 1,),
        in_specs=pair
        + [
            pl.BlockSpec((m, s, 2 * BL), lambda g: (0, 0, g + 1)),
            pl.BlockSpec((s, 2 * BL), lambda g: (0, g + 1)),
            pl.BlockSpec((1, 2 * BL), lambda g: (0, g + 1)),
            whole(s, s),
            whole(blocks, cap),
        ],
        out_specs=[
            pl.BlockSpec((2, rows + extra, BL), lambda g: (g + 1, 0, 0)),
            pl.BlockSpec((2, rows, BL), lambda g: (g + 1, 0, 0)),
            whole(4 * blocks, BL),
        ],
        out_shape=[near, far, jax.ShapeDtypeStruct((4 * blocks, BL), jnp.float32)],
        scratch_shapes=[mix3, carry],
        compiler_params=pltpu.CompilerParams(vmem_limit_bytes=VMEM_LIMIT),
        name="inner",
    )(*routing, *routing, mixing, slots)
    return pl.pallas_call(
        outer_kernel,
        grid=(1,),
        in_specs=pair + [whole(s, s), whole(blocks, cap), whole(2, m, s, BL), whole(4 * blocks, BL), held, held],
        out_specs=[held, held],
        out_shape=[near, far],
        scratch_shapes=[
            mix3,
            carry,
            pltpu.VMEM((2,) + near.shape[1:], jnp.float32),
            pltpu.VMEM((2,) + far.shape[1:], jnp.float32),
            pltpu.VMEM((4 * blocks, BL), jnp.float32),
            pltpu.VMEM((blocks - 2, 4 * blocks, BL), jnp.float32),
            pltpu.SemaphoreType.DMA((3,)),
        ],
        input_output_aliases={7: 0, 8: 1},
        compiler_params=pltpu.CompilerParams(vmem_limit_bytes=VMEM_LIMIT),
        name="outer",
    )(*routing, mixing, slots, halo, moments, near_part, far_part)


def member_order(runs, m, turned):
    rows = lax.broadcasted_iota(jnp.int32, (runs, runs), 0)
    cols = lax.broadcasted_iota(jnp.int32, (runs, runs), 1)
    reversed_rows = runs - m - rows + 2 * (rows % m)
    return (jnp.where(turned == 1, reversed_rows, rows) == cols).astype(jnp.float32)


def innovation_kernel(
    place_ref, count_ref, near_ref, values_ref, errors_ref, gram_ref, sums_ref
):
    blocks, cap = values_ref.shape
    sources = near_ref.shape[0]
    m = (near_ref.shape[1] - 4 * blocks) // 2
    runs = sources * m
    joined = lambda at, size: jnp.concatenate(
        [near_ref[:, at : at + size, :], near_ref[:, at + size : at + 2 * size, :]], axis=2
    )
    means = joined(2 * m, blocks)
    mean = jnp.sum(means, axis=0) * (1.0 / sources)
    drift = means - mean[None]
    moment = jnp.sum(joined(2 * m + 2 * blocks, blocks), axis=0) + m * jnp.sum(drift * drift, axis=0)
    spread = moment / (runs - 1)
    lanes = lax.broadcasted_iota(jnp.int32, (blocks, cap), 1)
    rows = lax.broadcasted_iota(jnp.int32, (blocks, cap), 0)
    counts = jnp.zeros((blocks, cap), jnp.int32)
    for k in range(blocks):
        counts = jnp.where(rows == k, count_ref[k], counts)
    live = (lanes < counts).astype(jnp.float32)
    departure = values_ref[...] - mean
    errors = errors_ref[...]
    terms = live * departure * departure / (errors * errors + spread)
    statistic = jnp.sum(jnp.sum(terms, axis=0, keepdims=True), axis=1, keepdims=True)
    total = jnp.sum(counts[:, :1].astype(jnp.float32), axis=0, keepdims=True)
    lanes = lax.broadcasted_iota(jnp.int32, sums_ref.shape, 1)
    sums_ref[...] = jnp.where(lanes < 64, statistic, total)

    own = lax.shift_right_logical(place_ref[0], 1)
    seen = dot(member_order(runs, m, place_ref[0] & 1), joined(0, m).reshape(runs, cap))
    mean = jnp.sum(seen, axis=0, keepdims=True) * (1.0 / runs)
    pert = seen - mean
    errors = errors_ref[pl.ds(own, 1), :]
    lanes = lax.broadcasted_iota(jnp.int32, (1, cap), 1)
    live = (lanes < count_ref[own]).astype(jnp.float32)
    weighted = pert * (live / (errors * errors))
    departure = values_ref[pl.ds(own, 1), :] - mean
    gram_ref[:runs, :] = dot(weighted, pert, NT)
    gram_ref[runs:, :] = dot(jnp.broadcast_to(departure, (8, cap)), weighted, NT)


def innovations(place, near, values, errors, counts, m):
    blocks, cap = values.shape
    sources, rows, lanes = near.shape
    extra = 2 * m + 4 * blocks
    runs = sources * m
    whole = lambda *shape: pl.BlockSpec(shape, lambda g: (0,) * len(shape))
    smem = pl.BlockSpec(memory_space=pltpu.SMEM)
    return pl.pallas_call(
        innovation_kernel,
        grid=(1,),
        in_specs=[
            smem,
            smem,
            pl.BlockSpec((sources, extra, lanes), lambda g: (0, rows // extra - 1, 0)),
            whole(blocks, cap),
            whole(blocks, cap),
        ],
        out_specs=[whole(runs + 8, runs), whole(8, 128)],
        out_shape=[
            jax.ShapeDtypeStruct((runs + 8, runs), jnp.float32),
            jax.ShapeDtypeStruct((8, 128), jnp.float32),
        ],
        name="innovation",
    )(place, counts, near, values, errors)


def small_inverse_factor(a):
    n = a.shape[0]
    rows = lax.broadcasted_iota(jnp.int32, (n, n), 0)
    cols = lax.broadcasted_iota(jnp.int32, (n, n), 1)
    both = jnp.concatenate([a, (rows == cols).astype(jnp.float32)], axis=1)
    groups = [both[k : k + 8] for k in range(0, n, 8)]
    sub = lax.broadcasted_iota(jnp.int32, (8, 2 * n), 0)
    lane = lambda x, j: jnp.broadcast_to(x[:, j : j + 1], x.shape)
    line = lambda x, i: jnp.broadcast_to(x[i : i + 1], x.shape)
    scales = []
    for j in range(0, n, 2):
        k, i = divmod(j, 8)
        head = groups[k]
        first = [lane(g, j) for g in groups[k:]]
        second = [lane(g, j + 1) for g in groups[k:]]
        p, q, t = line(first[0], i), line(second[0], i), line(second[0], i + 1)
        top, bottom = line(head, i), line(head, i + 1)
        scale_top = 1.0 / p
        scale_bottom = p * (1.0 / (p * t - q * q))
        slope = q * scale_top
        bottom = bottom - slope * top
        bottom_row = bottom * scale_bottom
        top_row = top * scale_top - slope * bottom_row
        groups[k:] = [
            g - f * top_row - h * bottom_row for g, f, h in zip(groups[k:], first, second)
        ]
        groups[k] = jnp.where(sub > i + 1, groups[k], jnp.where(sub == i + 1, bottom, head))
        if i == 0:
            scales.append(scale_top)
        scales[k] = jnp.where(sub > i, scale_bottom, jnp.where(sub == i, scale_top, scales[k]))
    inverse = jnp.concatenate([g * jnp.sqrt(c) for g, c in zip(groups, scales)], axis=0)
    return inverse[:, n:]


def inverse_factor(a):
    n = a.shape[0]
    if n <= 64:
        return small_inverse_factor(a)
    h = n // 2
    first = inverse_factor(a[:h, :h])
    cross = dot(a[h:, :h], first, NT)
    second = inverse_factor(a[h:, h:] - dot(cross, cross, NT))
    lower = -dot(second, dot(cross, first))
    zero = jnp.zeros((h, h), jnp.float32)
    return jnp.concatenate(
        [jnp.concatenate([first, zero], axis=1), jnp.concatenate([lower, second], axis=1)], axis=0
    )


def mixer_kernel(m, place_ref, gram_ref, sums_ref, mixer_ref):
    runs = gram_ref.shape[1]
    inflation = 0.5 + sums_ref[0:1, 0:1] / sums_ref[0:1, 64:65]
    rows = lax.broadcasted_iota(jnp.int32, (runs, runs), 0)
    cols = lax.broadcasted_iota(jnp.int32, (runs, runs), 1)
    system = gram_ref[:runs, :] + jnp.where(rows == cols, (runs - 1) / inflation, 0.0)
    inverse = inverse_factor(system)
    half_way = dot(gram_ref[runs:, :], inverse, NT)
    mean_weight = dot(half_way, inverse)
    mixer = mean_weight[0:1] + jnp.sqrt(jnp.float32(runs - 1)) * inverse
    turned = place_ref[0] & 1
    mixer = dot(mixer, member_order(runs, m, turned), NT)
    groups = runs // m
    for g in range(groups):
        spot = jnp.where(turned == 1, groups - 1 - g, g)
        mixer_ref[pl.ds(pl.multiple_of(spot * m, m), m), :] = mixer[g * m : (g + 1) * m]


def mixer_of(place, gram, sums, m):
    vmem = pl.BlockSpec(memory_space=pltpu.VMEM)
    return pl.pallas_call(
        functools.partial(mixer_kernel, m),
        in_specs=[pl.BlockSpec(memory_space=pltpu.SMEM)] + [vmem] * 2,
        out_specs=vmem,
        out_shape=jax.ShapeDtypeStruct((gram.shape[1],) * 2, jnp.float32),
        compiler_params=pltpu.CompilerParams(vmem_limit_bytes=SMALL_LIMIT),
        name="mixer",
    )(place, gram, sums)


def apply_kernel(mixer_ref, near_ref, far_ref, out_ref):
    sources, half, states, lanes = near_ref.shape
    runs = 2 * sources * half
    high, low = halves(mixer_ref[...])
    wide = jnp.concatenate([high, low, high], axis=1)
    flat = lambda ref: ref.reshape(sources * half * states, lanes)
    near_rows, far_rows = flat(near_ref), flat(far_ref)
    out_rows = out_ref.reshape(runs * states, lanes)

    def members(s):
        parts = [
            rows[pl.ds(s, sources * half, stride=states), :].reshape(sources, half, lanes)
            for rows in (near_rows, far_rows)
        ]
        return jnp.concatenate(parts, axis=1).reshape(runs, lanes)

    for s in range(0, states, 2):
        x = jnp.concatenate([members(s), members(s + 1)], axis=1)
        mean = jnp.sum(x, axis=0, keepdims=True) * (1.0 / runs)
        x_high, x_low = halves(x - mean)
        out = mean + fast_dot(wide, jnp.concatenate([x_high, x_high, x_low], axis=0))
        for i in range(2):
            out_rows[pl.ds(s + i, runs, stride=states), :] = out[:, i * lanes : (i + 1) * lanes]


def apply_mixer(mixer, near, far, chunk=24):
    sources, half, states, lanes = far.shape
    runs = 2 * sources * half
    part = pl.BlockSpec((sources, half, chunk, lanes), lambda g: (0, 0, g, 0))
    return pl.pallas_call(
        apply_kernel,
        grid=(states // chunk,),
        in_specs=[pl.BlockSpec((runs, runs), lambda g: (0, 0)), part, part],
        out_specs=pl.BlockSpec((runs, chunk, lanes), lambda g: (0, g, 0)),
        out_shape=jax.ShapeDtypeStruct((runs, states, lanes), jnp.float32),
        compiler_params=pltpu.CompilerParams(vmem_limit_bytes=VMEM_LIMIT),
        name="apply",
    )(mixer, near, far)


def unpack_kernel(x_ref, out_ref, sems):
    copies = [
        pltpu.make_async_copy(x_ref.at[b], out_ref.at[:, :, pl.ds(b * BL, BL)], sems.at[b])
        for b in range(x_ref.shape[0])
    ]
    for copy in copies:
        copy.start()
    for copy in copies:
        copy.wait()


def unpack(x):
    blocks, m, s, lanes = x.shape
    return pl.pallas_call(
        unpack_kernel,
        in_specs=[pl.BlockSpec(memory_space=pltpu.VMEM)],
        out_specs=pl.BlockSpec(memory_space=pl.ANY),
        out_shape=jax.ShapeDtypeStruct((m, s, blocks * lanes), jnp.float32),
        scratch_shapes=[pltpu.SemaphoreType.DMA((blocks,))],
        compiler_params=pltpu.CompilerParams(vmem_limit_bytes=SMALL_LIMIT),
        name="unpack",
    )(x)


def exchange(x):
    size, reaches = lax.axis_size("mem"), lax.axis_size("reach")
    groups = [
        [(size - 1 - i if r % 2 else i) * reaches + r for i in range(size)] for r in range(reaches)
    ]
    return lax.all_to_all(
        x, ("mem", "reach"), split_axis=0, concat_axis=0, tiled=True, axis_index_groups=groups
    )


def butterfly_sum(x, axes):
    for axis in axes:
        size = lax.axis_size(axis)
        step = 1
        while step < size:
            x = x + lax.ppermute(x, axis, [(i, i ^ step) for i in range(size)])
            step *= 2
    return x


def on_device(
    ensemble,
    outgoing_fraction,
    mixing,
    downstream_position,
    obs_index,
    obs_value,
    obs_error,
    obs_count,
):
    m, s, r = ensemble.shape
    blocks = r // BL
    reaches = lax.axis_size("reach")
    mem = lax.axis_index("mem").astype(jnp.int32)
    turned = (lax.axis_index("reach") % 2).astype(jnp.int32)
    block = jnp.where(turned == 1, lax.axis_size("mem") - 1 - mem, mem)
    place = (2 * block + turned).reshape(1)
    routing = (ensemble, outgoing_fraction, downstream_position.reshape(1, r), mixing)
    halo = lax.ppermute(edge_carries(*routing), "reach", [(i, i + 1) for i in range(reaches - 1)])
    near, far = forecast(*routing, obs_index, halo)

    near = exchange(near)
    far = exchange(far)
    gram, sums = innovations(place, near, obs_value, obs_error, obs_count, m)
    sums = butterfly_sum(sums, ("reach",))
    mixer = mixer_of(place, gram, sums, m)
    updated = apply_mixer(mixer, near.reshape(blocks, -1, s, BL), far.reshape(blocks, -1, s, BL))
    returned = exchange(updated.reshape(blocks, m, s, BL))
    return unpack(returned)


def solution(mesh):
    placed = (
        P("mem", None, "reach"),
        P(None, "reach"),
        P(),
        P("reach"),
        P("reach", None),
        P("reach", None),
        P("reach", None),
        P("reach"),
    )
    return jax.shard_map(
        on_device, mesh=mesh, in_specs=placed, out_specs=P("mem", None, "reach"), check_vma=False
    )
```
